512 devices in a mesh: grp: 32 (over x, z_lo, core), sp: 16 (over y, z_hi).
Axes of the slice: x: 4, y: 8, z: 8 (z_hi: 2, z_lo: 4; z = z_hi * 4 + z_lo), core: 2. Of those that a mesh axis runs over, the one named last changes fastest.
Arguments:
- queries: bfloat16 [65536, 4096], P(('grp', 'sp')), may hold values from -60 to 60
- keys: bfloat16 [65536, 512], P(('grp', 'sp')), may hold values from -60 to 60
- values: bfloat16 [65536, 512], P(('grp', 'sp')), may hold values from -6 to 6
- grad_out: bfloat16 [65536, 4096], P(('grp', 'sp')), may hold values from -40 to 40
- gain_q: float32 [128], replicated, may hold values from 0.5 to 6
- gain_k: float32 [128], replicated, may hold values from 0.5 to 6
- doc_ids: int32 [65536], P(('grp', 'sp')), may hold values from 0 to 1023, never falling along the last dimension, each value on 1 to 128 neighbouring positions
- bucket_len: int32 [32], P('grp'), may hold values from 512 to 2048, as said below
Outputs:
- grad_queries: bfloat16 [65536, 4096], P(('grp', 'sp'))
- grad_keys: bfloat16 [65536, 512], P(('grp', 'sp'))
- grad_values: bfloat16 [65536, 512], P(('grp', 'sp'))
- grad_gain_q: float32 [128], replicated
- grad_gain_k: float32 [128], replicated
The draws below stay inside these ranges and needn't reach their ends.
Inputs may be any that keep to these rules, and one draw needn't show every extreme that they name: `doc_ids`: ids never fall along the tokens; a document has at most 128 tokens and may run across buckets. Slots at positions from bucket_len on are padding. Some bucket is full and some holds 512 tokens.
All inputs are finite; a program needn't handle non-finite values.
Results may differ from the reference program's by a relative error of at most 0.006.
The reference program's roundings to bfloat16 on the way (of `query_norm`, `key_norm`, `attention_low` and `grad_scores`) count: a program that leaves them out, or rounds other values in their place, can miss the bound.
Values may be sent and summed in bfloat16 or wider, within the bound.
A program may use at most 128 MiB of HBM per device.

```python
import math
from functools import partial
import jax
import jax.numpy as jnp
import numpy as np
from jax import lax

HQ = 32
HK = 4
DH = 128
BUCKET = 2048
TOKENS = 65536
DOC_MOST = 128
DOCS = 1024


def shared_keys(key):
    return jax.random.normal(key, (TOKENS, HK * DH), jnp.float32)


def draw_queries(key, part):
    key = jax.random.fold_in(key, 21)
    first_key = jax.random.fold_in(key, 0)
    fresh = jax.random.normal(first_key, (TOKENS, HQ * DH), jnp.float32)
    result = fresh
    return jnp.clip(result, -60.0, 60.0).astype(jnp.bfloat16)


def draw_keys(key, part):
    base_keys = shared_keys(key)
    result = base_keys
    return jnp.clip(result, -60.0, 60.0).astype(jnp.bfloat16)


def draw_grad_out(key, part):
    key = jax.random.fold_in(key, 23)
    first_key = jax.random.fold_in(key, 0)
    rising = (3.0 ** (jnp.arange(TOKENS, dtype=jnp.float32) / TOKENS))[:, None]
    noise = jax.random.normal(first_key, (TOKENS, HQ * DH), jnp.float32)
    result = noise * rising
    return jnp.clip(result, -40.0, 40.0).astype(jnp.bfloat16)


def gain_values(key, lower, upper):
    return jax.random.uniform(key, (DH,), jnp.float32, lower, upper)


def draw_gain_q(key, part):
    key = jax.random.fold_in(key, 24)
    return gain_values(key, 0.6, 1.6)


def draw_gain_k(key, part):
    key = jax.random.fold_in(key, 25)
    return gain_values(key, 0.6, 1.6)


def draw_bucket_len(key, part):
    key = jax.random.fold_in(key, 26)
    first_key, second_key = jax.random.split(key)
    groups = TOKENS // BUCKET
    lengths = jax.random.randint(first_key, (groups,), BUCKET // 4, BUCKET + 1, jnp.int32)
    order = jax.random.permutation(second_key, groups)
    lengths = lengths.at[order[0]].set(BUCKET).at[order[1]].set(BUCKET // 4)
    return lengths.astype(jnp.int32)


def block_scale(stream_key, dims, cuts, smallest, high):
    level = 1.0
    for dim, shards_of in cuts:
        heights = jax.random.uniform(jax.random.fold_in(jax.random.fold_in(stream_key, 6), dim), (shards_of,), jnp.float32, smallest / len(cuts), high / len(cuts))
        level = level * jnp.repeat(jnp.exp(heights), dims[dim] // shards_of).reshape((-1,) + (1,) * (len(dims) - 1 - dim))
    return level


def split_up(count, total, bound, slope):
    loads = [(1 << 20) // math.isqrt(grade ** slope) + 1 for grade in range(2, count + 1)]
    spare, holding = total - bound - (count - 1), [1] * (count - 1)
    while spare > 0:
        free = [i for i in range(count - 1) if holding[i] < bound]
        pool, left = sum([loads[i] for i in free]), spare
        for i in free:
            more = min(bound - holding[i], max(1, left * loads[i] // pool), spare)
            holding[i] = holding[i] + more
            spare = spare - more
    return np.array([bound] + holding)


def ragged(own_key, number_of, total, bound, lean):
    if number_of == 2:
        one = jax.random.randint(own_key, (), max(1, total - bound), min(bound, total - 1) + 1)
        return jnp.stack([one, total - one])
    sizes = jnp.asarray(split_up(number_of, total, bound, lean), jnp.int32)
    twos = (number_of - 1) // 2
    giver, taker = sizes[1:1 + 2 * twos:2], sizes[2:2 + 2 * twos:2]
    slack = jnp.minimum(giver - 1, bound - taker)
    passed = jax.random.randint(jax.random.fold_in(own_key, 1), (twos,), 0, 1 << 20) % (slack + 1)
    sizes = sizes.at[1:1 + 2 * twos:2].set(giver - passed).at[2:2 + 2 * twos:2].set(taker + passed)
    return sizes[jax.random.permutation(jax.random.fold_in(own_key, 2), number_of)]


def bell_draw(key, extent, width, bound, pieces=(), held_as=jnp.bfloat16):
    entries = jax.random.normal(key, extent, jnp.float32) * width
    if len(pieces) > 0:
        entries = block_scale(key, extent, pieces, -0.22, 0.18) * entries
    return jnp.clip(entries, min=-bound, max=bound).astype(held_as)


def setup_inputs(seed: int = 0) -> dict:
    arg_keys = jax.random.split(jax.random.key(seed), 9)
    queries = draw_queries(jax.random.fold_in(arg_keys[8], 71), 0)
    keys = draw_keys(jax.random.fold_in(arg_keys[8], 71), 0)
    values = bell_draw(arg_keys[2], (TOKENS, HK * DH), 1.0, 6.0, ((0, 512),))
    grad_out = draw_grad_out(jax.random.fold_in(arg_keys[8], 71), 0)
    gain_q = draw_gain_q(jax.random.fold_in(arg_keys[8], 71), 0)
    gain_k = draw_gain_k(jax.random.fold_in(arg_keys[8], 71), 0)
    doc_ids = jnp.searchsorted(jnp.cumsum(ragged(arg_keys[6], DOCS, TOKENS, DOC_MOST, 1)), jnp.arange(TOKENS), side="right").astype(jnp.int32)
    bucket_len = draw_bucket_len(jax.random.fold_in(arg_keys[8], 71), 0)
    return {"queries": queries, "keys": keys, "values": values, "grad_out": grad_out, "gain_q": gain_q, "gain_k": gain_k, "doc_ids": doc_ids, "bucket_len": bucket_len}


norm_eps = 1e-06
masked_score = -1e+30

def rms_factor(inputs):
    return lax.rsqrt(lax.optimization_barrier(jnp.mean(inputs * inputs, axis=-1, keepdims=True)) + norm_eps)

def norm_backward(inputs, factor, gain, upstream):
    scaled = gain * upstream
    inner_mean = lax.optimization_barrier(jnp.mean(scaled * inputs, axis=-1, keepdims=True))
    return factor * scaled - inputs * factor * factor * factor * inner_mean

def one_bucket(operands, gain_q, gain_k):
    queries, keys, values, grad_out, doc_ids, bucket_end = operands
    group_size = HQ // HK
    score_scale = DH ** (-0.5)
    query_float = queries.reshape(BUCKET, HQ, DH).astype(jnp.float32)
    query_factor = rms_factor(query_float)
    query_norm = (query_float * query_factor * gain_q).astype(jnp.bfloat16)
    key_float = keys.reshape(BUCKET, HK, DH).astype(jnp.float32)
    key_factor = rms_factor(key_float)
    key_norm = (key_float * key_factor * gain_k).astype(jnp.bfloat16)
    key_wide = jnp.repeat(key_norm, group_size, axis=1).astype(jnp.float32)
    value_wide = jnp.repeat(values.reshape(BUCKET, HK, DH), group_size, axis=1).astype(jnp.float32)
    grad_heads = grad_out.reshape(BUCKET, HQ, DH).astype(jnp.float32)
    block_rows = min(512, BUCKET)
    positions = jnp.arange(BUCKET, dtype=jnp.int32)
    key_grad = jnp.zeros((BUCKET, HQ, DH), jnp.float32)
    value_grad = jnp.zeros((BUCKET, HQ, DH), jnp.float32)
    query_blocks = []
    for block_index in range(BUCKET // block_rows):
        row_start = block_index * block_rows
        row_stop = row_start + block_rows
        query_part = query_norm[row_start:row_stop].astype(jnp.float32)
        key_part = key_wide[:row_stop]
        scores = jnp.einsum('qhd,khd->hqk', query_part, key_part) * score_scale
        allowed = (doc_ids[row_start:row_stop, None] == doc_ids[None, :row_stop]) & (positions[None, :row_stop] <= positions[row_start:row_stop, None])
        live_rows = (positions[row_start:row_stop] < bucket_end).astype(jnp.float32)[None, :, None]
        scores = jnp.where(allowed[None], scores, masked_score)
        highest = lax.optimization_barrier(jnp.max(scores, axis=-1, keepdims=True))
        weights = jnp.exp(scores - highest)
        attention = weights / lax.optimization_barrier(jnp.sum(weights, axis=-1, keepdims=True)) * live_rows
        grad_part = grad_heads[row_start:row_stop]
        grad_attention = jnp.einsum('qhd,khd->hqk', grad_part, value_wide[:row_stop])
        row_delta = lax.optimization_barrier(jnp.sum(attention * grad_attention, axis=-1, keepdims=True))
        grad_scores = lax.optimization_barrier((attention * (grad_attention - row_delta)).astype(jnp.bfloat16)).astype(jnp.float32)
        attention_low = lax.optimization_barrier(attention.astype(jnp.bfloat16)).astype(jnp.float32)
        query_blocks.append(jnp.einsum('hqk,khd->qhd', grad_scores, key_part) * score_scale)
        key_grad = key_grad.at[:row_stop].add(jnp.einsum('hqk,qhd->khd', grad_scores, query_part) * score_scale)
        value_grad = value_grad.at[:row_stop].add(jnp.einsum('hqk,qhd->khd', attention_low, grad_part))
    grad_qnorm = jnp.concatenate(query_blocks, axis=0)
    grad_knorm = key_grad.reshape(BUCKET, HK, group_size, DH).sum(axis=2)
    value_sum = value_grad.reshape(BUCKET, HK, group_size, DH).sum(axis=2)
    grad_queries = norm_backward(query_float, query_factor, gain_q, grad_qnorm).astype(jnp.bfloat16)
    grad_keys = norm_backward(key_float, key_factor, gain_k, grad_knorm).astype(jnp.bfloat16)
    grad_values = value_sum.astype(jnp.bfloat16)
    gain_q_part = lax.optimization_barrier(jnp.sum(grad_qnorm * query_float * query_factor, axis=(0, 1)))
    gain_k_part = lax.optimization_barrier(jnp.sum(grad_knorm * key_float * key_factor, axis=(0, 1)))
    return (grad_queries.reshape(BUCKET, HQ * DH), grad_keys.reshape(BUCKET, HK * DH), grad_values.reshape(BUCKET, HK * DH), gain_q_part, gain_k_part)

def reference(queries, keys, values, grad_out, gain_q, gain_k, doc_ids, bucket_len):
    groups = TOKENS // BUCKET
    stacked = (queries.reshape(groups, BUCKET, HQ * DH), keys.reshape(groups, BUCKET, HK * DH), values.reshape(groups, BUCKET, HK * DH), grad_out.reshape(groups, BUCKET, HQ * DH), doc_ids.reshape(groups, BUCKET), bucket_len)
    grad_queries, grad_keys, grad_values, gain_q_parts, gain_k_parts = lax.map(partial(one_bucket, gain_q=gain_q, gain_k=gain_k), stacked)
    total_scale = TOKENS ** (-0.5)
    return (grad_queries.reshape(TOKENS, HQ * DH), grad_keys.reshape(TOKENS, HK * DH), grad_values.reshape(TOKENS, HK * DH), lax.optimization_barrier(jnp.sum(gain_q_parts, axis=0)) * total_scale, lax.optimization_barrier(jnp.sum(gain_k_parts, axis=0)) * total_scale)
```

```python
import functools
import itertools
import math

import jax
import jax.numpy as jnp
from jax import lax
from jax.experimental import pallas as pl
from jax.experimental.pallas import tpu as pltpu
from jax.sharding import PartitionSpec as P

MESH = pl.DeviceIdType.MESH
F32 = jnp.float32
BF16 = jnp.bfloat16
eps = 1e-06
masked_score = -1e30
T = 128
HEADS = 32
KV = 4
GROUP = HEADS // KV
SPAN = dict(dx=4, dy=8, dz=8, dc=2)


def shifted(dx=0, dy=0, dz=0, dc=0):
    g, s = lax.axis_index("grp"), lax.axis_index("sp")
    x, y = g // 8, s // 2
    z, c = (s % 2) * 4 + (g // 2) % 4, g % 2
    x, y, z, c = (x + dx) % 4, (y + dy) % 8, (z + dz) % 8, (c + dc) % 2
    return (x * 8 + (z % 4) * 2 + c, y * 2 + z // 4)


def partners(axes):
    found = [
        dict(zip(axes, combo))
        for combo in itertools.product(*[range(SPAN[a]) for a in axes])
        if any(combo)
    ]

    def distance(d):
        return sum(min(v, SPAN[a] - v) for a, v in d.items() if a != "dc")

    return sorted(found, key=lambda d: -distance(d))


STAGES = (partners(("dc", "dz")), partners(("dx", "dy")))
PEERS = sum(len(s) for s in STAGES)


def contract(a, b, dims):
    return lax.dot_general(a, b, (dims, ((), ())), preferred_element_type=F32)


def kernel(
    q_hbm, k_hbm, v_hbm, g_hbm, gain_q_hbm, gain_k_hbm, doc_hbm, len_hbm,
    gq_out, gk_out, gv_out, gain_q_out, gain_k_out,
    q_in, g_in, k_in, v_in, gains, doc, length,
    k_halo, v_halo, doc_halo,
    qn, xhat, rfac, kn, kxhat, krfac, bias, live,
    dq, dk_own, dv_own, k_send, v_send, k_back, v_back, gq_stage,
    ar_send, ar_recv,
    in_sem, fwd_send, fwd_recv, ret_send, ret_recv, ars_sem, arr_sem, out_sem,
):
    sp = lax.axis_index("sp")
    grp = lax.axis_index("grp")
    has_prev, has_next = sp > 0, sp < 15
    early = sp % 2 == 0
    nxt, prv = (grp, (sp + 1) % 16), (grp, (sp + 15) % 16)
    scale = 1.0 / math.sqrt(T)

    barrier = pltpu.get_barrier_semaphore()

    def greet(d):
        pl.semaphore_signal(barrier, inc=1, device_id=d, device_id_type=MESH)

    @pl.when(has_next)
    def _():
        greet(nxt)

    @pl.when(has_prev)
    def _():
        greet(prv)

    for stage in STAGES:
        for d in stage:
            greet(shifted(**d))

    loads = [
        (k_hbm, k_in), (v_hbm, v_in), (doc_hbm, doc), (len_hbm, length),
        (gain_q_hbm, gains.at[pl.ds(0, 1)]), (gain_k_hbm, gains.at[pl.ds(1, 1)]),
    ]
    wide = GROUP * T
    for c in range(KV):
        cols = pl.ds(c * wide, wide)
        loads.append((q_hbm.at[:, cols], q_in.at[:, cols]))
        loads.append((g_hbm.at[:, cols], g_in.at[:, cols]))
    loads = [pltpu.make_async_copy(s, d, in_sem.at[i]) for i, (s, d) in enumerate(loads)]
    for cp in loads:
        cp.start()

    def forward(c):
        cols = pl.ds(c * T, T)
        return (
            pltpu.make_async_remote_copy(
                k_hbm.at[:, cols], k_halo.at[:, cols], fwd_send.at[2 * c], fwd_recv.at[2 * c],
                device_id=nxt, device_id_type=MESH,
            ),
            pltpu.make_async_remote_copy(
                v_hbm.at[:, cols], v_halo.at[:, cols], fwd_send.at[2 * c + 1],
                fwd_recv.at[2 * c + 1], device_id=nxt, device_id_type=MESH,
            ),
        )

    def doc_copy():
        return pltpu.make_async_remote_copy(
            doc_hbm, doc_halo, fwd_send.at[2 * KV], fwd_recv.at[2 * KV],
            device_id=nxt, device_id_type=MESH,
        )

    def open_and_send():
        near = has_next.astype(jnp.int32) + has_prev.astype(jnp.int32)
        pl.semaphore_wait(barrier, PEERS + near)

        @pl.when(has_next)
        def _():
            doc_copy().start()
            for c in range(KV):
                for cp in forward(c):
                    cp.start()

    @pl.when(jnp.logical_not(early))
    def _():
        open_and_send()

    for cp in loads[:6]:
        cp.wait()
    gain_q, gain_k = gains[0:1, :], gains[1:2, :]

    def factor(x):
        return lax.rsqrt(jnp.mean(x * x, axis=-1, keepdims=True) + eps)

    def norm_keys(raw, c, row):
        x = raw[:, c * T : (c + 1) * T].astype(F32)
        r = factor(x)
        xr = x * r
        kn[c, row : row + T, :] = (xr * gain_k).astype(BF16)
        kxhat[c, row : row + T, :] = xr
        return r

    for c in range(KV):
        krfac[c] = jnp.broadcast_to(norm_keys(k_in, c, T), (T, T))
    at_t = lax.broadcasted_iota(jnp.int32, (T, T), 1)
    at_s = lax.broadcasted_iota(jnp.int32, (T, T), 0)
    doc_t = jnp.broadcast_to(doc[...].astype(F32), (T, T))
    own = (doc_t == doc_t.T) & (at_s <= at_t)
    bias[T:, :] = jnp.where(own, 0.0, masked_score)
    place = sp * T + lax.broadcasted_iota(jnp.int32, (1, T), 1)
    live[...] = jnp.where(place < length[0], 1.0, 0.0)

    for c in range(KV):
        loads[6 + 2 * c].wait()
        loads[7 + 2 * c].wait()

        def norm_query(i, carry, c=c):
            h = c * GROUP + i
            cols = pl.ds(pl.multiple_of(h * T, T), T)
            x = q_in[:, cols].astype(F32)
            r = factor(x)
            xr = x * r
            qn[h] = (xr * gain_q).astype(BF16)
            xhat[h] = xr
            rfac[h] = jnp.broadcast_to(r, (T, T))
            return carry

        lax.fori_loop(0, GROUP, norm_query, 0, unroll=4)

    @pl.when(early)
    def _():
        open_and_send()

    @pl.when(has_prev)
    def _():
        doc_copy().wait_recv()

    @pl.when(jnp.logical_not(has_prev))
    def _():
        doc_halo[...] = jnp.zeros_like(doc_halo)
        k_halo[...] = jnp.zeros_like(k_halo)
        v_halo[...] = jnp.zeros_like(v_halo)

    doc_s = jnp.broadcast_to(doc_halo[...].astype(F32), (T, T)).T
    first = jnp.where(has_prev, 0.0, masked_score)
    bias[:T, :] = jnp.where(doc_s == doc_t, first, masked_score)

    def back(c):
        cols = pl.ds(c * T, T)
        return (
            pltpu.make_async_remote_copy(
                k_send.at[:, cols], k_back.at[:, cols], ret_send.at[2 * c], ret_recv.at[2 * c],
                device_id=prv, device_id_type=MESH,
            ),
            pltpu.make_async_remote_copy(
                v_send.at[:, cols], v_back.at[:, cols], ret_send.at[2 * c + 1],
                ret_recv.at[2 * c + 1], device_id=prv, device_id_type=MESH,
            ),
        )

    gain_q_sum = jnp.zeros((T, T), F32)
    gain_k_sum = jnp.zeros((2 * T, T), F32)
    for c in range(KV):
        cols = slice(c * T, (c + 1) * T)

        @pl.when(has_prev)
        def _(c=c):
            for cp in forward(c):
                cp.wait_recv()

        norm_keys(k_halo, c, 0)
        key = kn[c]
        value = jnp.concatenate([v_halo[:, cols], v_in[:, cols]], axis=0)

        def pair(i, carry, c=c, key=key, value=value):
            dk, dv, gq_sum = carry
            h = c * GROUP + 2 * i
            query = jnp.concatenate([qn[h], qn[h + 1]], axis=0)
            col0 = pl.ds(pl.multiple_of(h * T, T), T)
            col1 = pl.ds(pl.multiple_of(h * T + T, T), T)
            grad = jnp.concatenate([g_in[:, col0], g_in[:, col1]], axis=0)
            both = jnp.concatenate([bias[...], bias[...]], axis=1)
            score = contract(key, query, ((1,), (1,))) + both
            high = jnp.max(score, axis=0, keepdims=True)
            weight = jnp.exp((score - high) * scale)
            total = jnp.sum(weight, axis=0, keepdims=True)
            alive = jnp.concatenate([live[...], live[...]], axis=1)
            att = weight * (alive / total)
            gatt = contract(value, grad, ((1,), (1,)))
            delta = jnp.sum(att * gatt, axis=0, keepdims=True)
            ds = (att * (gatt - delta)).astype(BF16)
            dk = dk + contract(ds, query, ((1,), (0,)))
            dv = dv + contract(att.astype(BF16), grad, ((1,), (0,)))
            dq2 = contract(ds, key, ((0,), (0,))) * scale
            dq[h] = dq2[:T]
            dq[h + 1] = dq2[T:]
            gq_sum = gq_sum + dq2[:T] * xhat[h] + dq2[T:] * xhat[h + 1]
            return dk, dv, gq_sum

        zero = jnp.zeros((2 * T, T), F32)
        dk, dv, gain_q_sum = lax.fori_loop(0, GROUP // 2, pair, (zero, zero, gain_q_sum), unroll=2)
        dk = dk * scale
        gain_k_sum = gain_k_sum + dk * kxhat[c]
        dk_own[:, cols] = dk[T:]
        dv_own[:, cols] = dv[T:]
        k_send[:, cols] = dk[:T].astype(BF16)
        v_send[:, cols] = dv[:T].astype(BF16)

        @pl.when(has_prev)
        def _(c=c):
            for cp in back(c):
                cp.start()

    sums = jnp.concatenate(
        [
            jnp.sum(gain_q_sum, axis=0, keepdims=True),
            jnp.sum(gain_k_sum, axis=0, keepdims=True),
            jnp.zeros((6, T), F32),
        ],
        axis=0,
    )

    def exchange(stage):
        base = sum(len(s) for s in STAGES[:stage])
        return [
            pltpu.make_async_remote_copy(
                ar_send.at[stage], ar_recv.at[base + i], ars_sem.at[base + i],
                arr_sem.at[base + i], device_id=shifted(**d), device_id_type=MESH,
            )
            for i, d in enumerate(STAGES[stage])
        ]

    def gather_sums(stage, sums):
        base = sum(len(s) for s in STAGES[:stage])
        for i, cp in enumerate(exchange(stage)):
            cp.wait_recv()
            sums = sums + ar_recv[base + i]
        return sums

    ar_send[0] = sums
    for cp in exchange(0):
        cp.start()

    def backward(xr, r, gain, up):
        u = gain * up
        return r * (u - xr * jnp.mean(u * xr, axis=-1, keepdims=True))

    writes = []
    for c in range(KV):

        def query_grad(i, carry, c=c):
            h = c * GROUP + i
            cols = pl.ds(pl.multiple_of(h * T, T), T)
            gq_stage[:, cols] = backward(xhat[h], rfac[h], gain_q, dq[h]).astype(BF16)
            return carry

        lax.fori_loop(0, GROUP, query_grad, 0, unroll=4)
        cols = pl.ds(c * wide, wide)
        cp = pltpu.make_async_copy(gq_stage.at[:, cols], gq_out.at[:, cols], out_sem.at[c])
        cp.start()
        writes.append(cp)

    sums = gather_sums(0, sums)
    ar_send[1] = sums
    for cp in exchange(1):
        cp.start()

    for c in range(KV):
        cols = slice(c * T, (c + 1) * T)

        @pl.when(has_next)
        def _(c=c, cols=cols):
            for cp in back(c):
                cp.wait_recv()
            dk_own[:, cols] = dk_own[:, cols] + k_back[:, cols].astype(F32)
            dv_own[:, cols] = dv_own[:, cols] + v_back[:, cols].astype(F32)

        gk_out[:, cols] = backward(kxhat[c, T:, :], krfac[c], gain_k, dk_own[:, cols]).astype(BF16)
        gv_out[:, cols] = dv_own[:, cols].astype(BF16)

    sums = gather_sums(1, sums) * (1.0 / math.sqrt(T * 512))
    gain_q_out[...] = sums[0:1, :]
    gain_k_out[...] = sums[1:2, :]

    @pl.when(has_next)
    def _():
        doc_copy().wait_send()
        for c in range(KV):
            for cp in forward(c):
                cp.wait_send()

    @pl.when(has_prev)
    def _():
        for c in range(KV):
            for cp in back(c):
                cp.wait_send()

    for stage in range(len(STAGES)):
        for cp in exchange(stage):
            cp.wait_send()
    for cp in writes:
        cp.wait()


def body(queries, keys, values, grad_out, gain_q, gain_k, doc_ids, bucket_len):
    anywhere = pl.BlockSpec(memory_space=pl.ANY)
    vmem = pl.BlockSpec(memory_space=pltpu.VMEM)
    wide, narrow = queries.shape, keys.shape
    dma = pltpu.SemaphoreType.DMA
    outs = pl.pallas_call(
        kernel,
        out_shape=(
            jax.ShapeDtypeStruct(wide, BF16),
            jax.ShapeDtypeStruct(narrow, BF16),
            jax.ShapeDtypeStruct(narrow, BF16),
            jax.ShapeDtypeStruct((1, T), F32),
            jax.ShapeDtypeStruct((1, T), F32),
        ),
        in_specs=[anywhere] * 8,
        out_specs=(anywhere, vmem, vmem, vmem, vmem),
        scratch_shapes=[
            pltpu.VMEM(wide, BF16), pltpu.VMEM(wide, BF16),
            pltpu.VMEM(narrow, BF16), pltpu.VMEM(narrow, BF16),
            pltpu.VMEM((2, T), F32), pltpu.VMEM((1, T), jnp.int32), pltpu.SMEM((1,), jnp.int32),
            pltpu.VMEM(narrow, BF16), pltpu.VMEM(narrow, BF16), pltpu.VMEM((1, T), jnp.int32),
            pltpu.VMEM((HEADS, T, T), BF16), pltpu.VMEM((HEADS, T, T), F32),
            pltpu.VMEM((HEADS, T, T), F32),
            pltpu.VMEM((KV, 2 * T, T), BF16), pltpu.VMEM((KV, 2 * T, T), F32),
            pltpu.VMEM((KV, T, T), F32),
            pltpu.VMEM((2 * T, T), F32), pltpu.VMEM((1, T), F32),
            pltpu.VMEM((HEADS, T, T), F32),
            pltpu.VMEM(narrow, F32), pltpu.VMEM(narrow, F32),
            pltpu.VMEM(narrow, BF16), pltpu.VMEM(narrow, BF16),
            pltpu.VMEM(narrow, BF16), pltpu.VMEM(narrow, BF16),
            pltpu.VMEM(wide, BF16),
            pltpu.VMEM((2, 8, T), F32), pltpu.VMEM((PEERS, 8, T), F32),
            dma((14,)), dma((9,)), dma((9,)), dma((8,)), dma((8,)),
            dma((PEERS,)), dma((PEERS,)), dma((KV,)),
        ],
        compiler_params=pltpu.CompilerParams(
            collective_id=0, has_side_effects=True, vmem_limit_bytes=60 * 2**20
        ),
    )(
        queries, keys, values, grad_out, gain_q.reshape(1, T), gain_k.reshape(1, T),
        doc_ids.reshape(1, T), bucket_len,
    )
    return outs[0], outs[1], outs[2], outs[3].reshape(T), outs[4].reshape(T)


def solution(mesh):
    rows = P(("grp", "sp"), None)
    return jax.shard_map(
        body,
        mesh=mesh,
        in_specs=(rows, rows, rows, rows, P(), P(), P(("grp", "sp")), P("grp")),
        out_specs=(rows, rows, rows, P(), P()),
        check_vma=False,
    )
```

```python
import functools
import math

import jax
import jax.numpy as jnp
from jax import lax
from jax.experimental import pallas as pl
from jax.experimental.pallas import tpu as pltpu
from jax.sharding import PartitionSpec as P

MESH = pl.DeviceIdType.MESH
F32 = jnp.float32
BF16 = jnp.bfloat16
eps = 1e-06
masked_score = -1e30
T = 128
HEADS = 32
KV = 4
GROUP = HEADS // KV
STAGES = 3
SIDE = 8
EARLY = 0
PARTS = 4


def ring(value, step, size):
    return lax.rem(value + step, size)


def places():
    g, s = lax.axis_index("grp"), lax.axis_index("sp")
    x, z_lo, c = lax.div(g, 8), lax.rem(lax.div(g, 2), 4), lax.rem(g, 2)
    y, z_hi = lax.div(s, 2), lax.rem(s, 2)

    def along_z(z):
        return (x * 8 + lax.rem(z, 4) * 2 + c, y * 2 + lax.div(z, 4))

    def along_y(at):
        return (g, at * 2 + z_hi)

    def along_xc(at):
        return (lax.div(at, 2) * 8 + z_lo * 2 + lax.rem(at, 2), s)

    return ((z_hi * 4 + z_lo, along_z), (y, along_y), (x * 2 + c, along_xc))


def contract(a, b, dims):
    return lax.dot_general(a, b, (dims, ((), ())), preferred_element_type=F32)


def kernel(
    q_hbm, k_hbm, v_hbm, g_hbm, gain_q_hbm, gain_k_hbm, doc_hbm, len_hbm,
    gq_out, gk_out, gv_out, gain_out,
    q_in, g_in, k_in, v_in, gains, doc, length,
    k_halo, v_halo, doc_halo,
    qn, xhat, rfac, kn, kxhat, krfac, bias, live,
    dq, dk_own, dv_own, k_send, v_send, k_back, v_back, gq_stage,
    ar_send, ar_recv,
    in_sem, fwd_send, fwd_recv, ret_send, ret_recv, ars_sem, arr_sem, out_sem,
):
    sp = lax.axis_index("sp")
    grp = lax.axis_index("grp")
    has_prev, has_next = sp > 0, sp < 15
    early = sp % 2 == 0
    nxt, prv = (grp, (sp + 1) % 16), (grp, (sp + 15) % 16)
    scale = 1.0 / math.sqrt(T)

    barrier = pltpu.get_barrier_semaphore()

    def greet(d):
        pl.semaphore_signal(barrier, inc=1, device_id=d, device_id_type=MESH)

    @pl.when(has_next)
    def _():
        greet(nxt)

    @pl.when(has_prev)
    def _():
        greet(prv)

    rows = places()
    for here, device in rows:
        for step in (4, 3, 5, 2, 6, 1, 7):
            greet(device(ring(here, step, SIDE)))

    loads = [
        (k_hbm, k_in), (v_hbm, v_in), (doc_hbm, doc), (len_hbm, length),
        (gain_q_hbm, gains.at[pl.ds(0, 1)]), (gain_k_hbm, gains.at[pl.ds(1, 1)]),
    ]
    wide = GROUP * T
    for c in range(KV):
        cols = pl.ds(c * wide, wide)
        loads.append((q_hbm.at[:, cols], q_in.at[:, cols]))
        loads.append((g_hbm.at[:, cols], g_in.at[:, cols]))
    loads = [pltpu.make_async_copy(s, d, in_sem.at[i]) for i, (s, d) in enumerate(loads)]
    for cp in loads:
        cp.start()

    def forward(c):
        cols = pl.ds(c * T, T)
        return (
            pltpu.make_async_remote_copy(
                k_hbm.at[:, cols], k_halo.at[:, cols], fwd_send.at[2 * c], fwd_recv.at[2 * c],
                device_id=nxt, device_id_type=MESH,
            ),
            pltpu.make_async_remote_copy(
                v_hbm.at[:, cols], v_halo.at[:, cols], fwd_send.at[2 * c + 1],
                fwd_recv.at[2 * c + 1], device_id=nxt, device_id_type=MESH,
            ),
        )

    def doc_copy():
        return pltpu.make_async_remote_copy(
            doc_hbm, doc_halo, fwd_send.at[2 * KV], fwd_recv.at[2 * KV],
            device_id=nxt, device_id_type=MESH,
        )

    def open_and_send():
        near = has_next.astype(jnp.int32) + has_prev.astype(jnp.int32)
        pl.semaphore_wait(barrier, STAGES * (SIDE - 1) + near)

        @pl.when(has_next)
        def _():
            doc_copy().start()
            for c in range(KV):
                for cp in forward(c):
                    cp.start()

    @pl.when(jnp.logical_not(early))
    def _():
        open_and_send()

    for cp in loads[:6]:
        cp.wait()
    gain_q, gain_k = gains[0:1, :], gains[1:2, :]

    def factor(x):
        return lax.rsqrt(jnp.mean(x * x, axis=-1, keepdims=True) + eps)

    def norm_keys(raw, c, row):
        x = raw[:, c * T : (c + 1) * T].astype(F32)
        r = factor(x)
        xr = x * r
        kn[c, row : row + T, :] = (xr * gain_k).astype(BF16)
        kxhat[c, row : row + T, :] = xr
        return r

    for c in range(KV):
        krfac[c] = jnp.broadcast_to(norm_keys(k_in, c, T), (T, T))
    at_t = lax.broadcasted_iota(jnp.int32, (T, T), 1)
    at_s = lax.broadcasted_iota(jnp.int32, (T, T), 0)
    doc_t = jnp.broadcast_to(doc[...].astype(F32), (T, T))
    own = (doc_t == doc_t.T) & (at_s <= at_t)
    bias[T:, :] = jnp.where(own, 0.0, masked_score)
    place = sp * T + lax.broadcasted_iota(jnp.int32, (1, T), 1)
    live[...] = jnp.where(place < length[...], 1.0, 0.0)

    for c in range(KV):
        loads[6 + 2 * c].wait()
        loads[7 + 2 * c].wait()

        def norm_query(i, carry, c=c):
            h = c * GROUP + i
            cols = pl.ds(pl.multiple_of(h * T, T), T)
            x = q_in[:, cols].astype(F32)
            r = factor(x)
            xr = x * r
            qn[h] = (xr * gain_q).astype(BF16)
            xhat[h] = xr
            rfac[h] = jnp.broadcast_to(r, (T, T))
            return carry

        lax.fori_loop(0, GROUP, norm_query, 0, unroll=4)

    @pl.when(early)
    def _():
        open_and_send()

    @pl.when(has_prev)
    def _():
        doc_copy().wait_recv()

    @pl.when(jnp.logical_not(has_prev))
    def _():
        doc_halo[...] = jnp.zeros_like(doc_halo)
        k_halo[...] = jnp.zeros_like(k_halo)
        v_halo[...] = jnp.zeros_like(v_halo)

    doc_s = jnp.broadcast_to(doc_halo[...].astype(F32), (T, T)).T
    first = jnp.where(has_prev, 0.0, masked_score)
    bias[:T, :] = jnp.where(doc_s == doc_t, first, masked_score)

    def back(c):
        cols = pl.ds(c * T, T)
        return (
            pltpu.make_async_remote_copy(
                k_send.at[:, cols], k_back.at[:, cols], ret_send.at[2 * c], ret_recv.at[2 * c],
                device_id=prv, device_id_type=MESH,
            ),
            pltpu.make_async_remote_copy(
                v_send.at[:, cols], v_back.at[:, cols], ret_send.at[2 * c + 1],
                ret_recv.at[2 * c + 1], device_id=prv, device_id_type=MESH,
            ),
        )

    gain_q_sum = jnp.zeros((T, T), F32)
    gain_k_sum = jnp.zeros((2 * T, T), F32)
    for c in range(KV):
        cols = slice(c * T, (c + 1) * T)

        @pl.when(has_prev)
        def _(c=c):
            for cp in forward(c):
                cp.wait_recv()

        norm_keys(k_halo, c, 0)
        key = kn[c]
        value = jnp.concatenate([v_halo[:, cols], v_in[:, cols]], axis=0)

        def pair(i, carry, c=c, key=key, value=value):
            dk, dv, gq_sum = carry
            h = c * GROUP + 2 * i
            query = jnp.concatenate([qn[h], qn[h + 1]], axis=0)
            col0 = pl.ds(pl.multiple_of(h * T, T), T)
            col1 = pl.ds(pl.multiple_of(h * T + T, T), T)
            grad = jnp.concatenate([g_in[:, col0], g_in[:, col1]], axis=0)
            both = jnp.concatenate([bias[...], bias[...]], axis=1)
            score = contract(key, query, ((1,), (1,))) + both
            high = jnp.max(score, axis=0, keepdims=True)
            weight = jnp.exp((score - high) * scale)
            total = jnp.sum(weight, axis=0, keepdims=True)
            alive = jnp.concatenate([live[...], live[...]], axis=1)
            att = weight * (alive / total)
            gatt = contract(value, grad, ((1,), (1,)))
            delta = jnp.sum(att * gatt, axis=0, keepdims=True)
            ds = (att * (gatt - delta)).astype(BF16)
            dk = dk + contract(ds, query, ((1,), (0,)))
            dv = dv + contract(att.astype(BF16), grad, ((1,), (0,)))
            dq2 = contract(ds, key, ((0,), (0,))) * scale
            dq[h] = dq2[:T]
            dq[h + 1] = dq2[T:]
            gq_sum = gq_sum + dq2[:T] * xhat[h] + dq2[T:] * xhat[h + 1]
            return dk, dv, gq_sum

        zero = jnp.zeros((2 * T, T), F32)
        dk, dv, gain_q_sum = lax.fori_loop(0, GROUP // 2, pair, (zero, zero, gain_q_sum), unroll=2)
        dk = dk * scale
        gain_k_sum = gain_k_sum + dk * kxhat[c]
        dk_own[:, cols] = dk[T:]
        dv_own[:, cols] = dv[T:]
        k_send[:, cols] = dk[:T].astype(BF16)
        v_send[:, cols] = dv[:T].astype(BF16)

        if c < EARLY:

            @pl.when(has_prev)
            def _(c=c):
                for cp in back(c):
                    cp.start()

    sums = jnp.concatenate(
        [
            jnp.sum(gain_q_sum, axis=0, keepdims=True),
            jnp.sum(gain_k_sum, axis=0, keepdims=True),
        ],
        axis=0,
    )

    def exchange(stage):
        here, device = rows[stage]
        return [
            pltpu.make_async_remote_copy(
                ar_send.at[stage], ar_recv.at[stage, here], ars_sem.at[stage, step - 1],
                arr_sem.at[stage, here], device_id=device(ring(here, step, SIDE)),
                device_id_type=MESH,
            )
            for step in (4, 3, 5, 2, 6, 1, 7)
        ]

    def send_sums(stage, sums):
        ar_send[stage] = sums
        ar_recv[stage, rows[stage][0]] = sums
        for cp in exchange(stage):
            cp.start()

    def gather_sums(stage):
        here, _ = rows[stage]
        for step in range(1, SIDE):
            at = ring(here, step, SIDE)
            pltpu.make_async_copy(
                ar_recv.at[stage, at], ar_recv.at[stage, at], arr_sem.at[stage, at]
            ).wait()
        total = ar_recv[stage, 0]
        for at in range(1, SIDE):
            total = total + ar_recv[stage, at]
        return total

    send_sums(0, sums)

    @pl.when(has_prev)
    def _():
        for c in range(EARLY, KV):
            for cp in back(c):
                cp.start()

    def backward(xr, r, gain, up):
        u = gain * up
        return r * (u - xr * jnp.mean(u * xr, axis=-1, keepdims=True))

    writes = []
    for c in range(KV):

        def query_grad(i, carry, c=c):
            h = c * GROUP + i
            cols = pl.ds(pl.multiple_of(h * T, T), T)
            gq_stage[:, cols] = backward(xhat[h], rfac[h], gain_q, dq[h]).astype(BF16)
            return carry

        lax.fori_loop(0, GROUP, query_grad, 0, unroll=4)
        cols = pl.ds(c * wide, wide)
        cp = pltpu.make_async_copy(gq_stage.at[:, cols], gq_out.at[:, cols], out_sem.at[c])
        cp.start()
        writes.append(cp)

    send_sums(1, gather_sums(0))

    send_sums(2, gather_sums(1))

    for c in range(KV):
        cols = slice(c * T, (c + 1) * T)

        @pl.when(has_next)
        def _(c=c, cols=cols):
            for cp in back(c):
                cp.wait_recv()
            dk_own[:, cols] = dk_own[:, cols] + k_back[:, cols].astype(F32)
            dv_own[:, cols] = dv_own[:, cols] + v_back[:, cols].astype(F32)

        gk_out[:, cols] = backward(kxhat[c, T:, :], krfac[c], gain_k, dk_own[:, cols]).astype(BF16)
        gv_out[:, cols] = dv_own[:, cols].astype(BF16)

    gain_out[...] = gather_sums(2) * (1.0 / math.sqrt(T * 512))

    @pl.when(has_next)
    def _():
        doc_copy().wait_send()
        for c in range(KV):
            for cp in forward(c):
                cp.wait_send()

    @pl.when(has_prev)
    def _():
        for c in range(KV):
            for cp in back(c):
                cp.wait_send()

    for stage in range(STAGES):
        for cp in exchange(stage):
            cp.wait_send()
    for cp in writes:
        cp.wait()


def hand_over(gq, gk, gv, gain, gq_out, gk_out, gv_out, gain_q_out, gain_k_out, wide, near, last, sem):
    pairs = [(gk, near.at[0], gk_out), (gv, near.at[1], gv_out)]
    pairs += [
        (gain.at[pl.ds(i, 1)], last.at[pl.ds(i, 1)], out)
        for i, out in enumerate((gain_q_out, gain_k_out))
    ]
    part = T // PARTS
    for i in range(PARTS):
        at = pl.ds(i * part, part)
        pairs.append((gq.at[at], wide.at[at], gq_out.at[at]))
    reads = [pltpu.make_async_copy(a, b, sem.at[0, i]) for i, (a, b, _) in enumerate(pairs)]
    writes = [pltpu.make_async_copy(b, c, sem.at[1, i]) for i, (_, b, c) in enumerate(pairs)]
    for cp in reads:
        cp.start()
    for read, write in zip(reads, writes):
        read.wait()
        write.start()
    for cp in writes:
        cp.wait()


def body(queries, keys, values, grad_out, gain_q, gain_k, doc_ids, bucket_len):
    hbm = pl.BlockSpec(memory_space=pltpu.HBM)
    vmem = pl.BlockSpec(memory_space=pltpu.VMEM)
    wide, narrow = queries.shape, keys.shape
    dma = pltpu.SemaphoreType.DMA
    outs = pl.pallas_call(
        kernel,
        out_shape=(
            jax.ShapeDtypeStruct(wide, BF16),
            jax.ShapeDtypeStruct(narrow, BF16),
            jax.ShapeDtypeStruct(narrow, BF16),
            jax.ShapeDtypeStruct((2, T), F32),
        ),
        in_specs=[hbm] * 8,
        out_specs=(hbm, vmem, vmem, vmem),
        scratch_shapes=[
            pltpu.VMEM(wide, BF16), pltpu.VMEM(wide, BF16),
            pltpu.VMEM(narrow, BF16), pltpu.VMEM(narrow, BF16),
            pltpu.VMEM((2, T), F32), pltpu.VMEM((1, T), jnp.int32), pltpu.VMEM((1, 1), jnp.int32),
            pltpu.VMEM(narrow, BF16), pltpu.VMEM(narrow, BF16), pltpu.VMEM((1, T), jnp.int32),
            pltpu.VMEM((HEADS, T, T), BF16), pltpu.VMEM((HEADS, T, T), F32),
            pltpu.VMEM((HEADS, T, T), F32),
            pltpu.VMEM((KV, 2 * T, T), BF16), pltpu.VMEM((KV, 2 * T, T), F32),
            pltpu.VMEM((KV, T, T), F32),
            pltpu.VMEM((2 * T, T), F32), pltpu.VMEM((1, T), F32),
            pltpu.VMEM((HEADS, T, T), F32),
            pltpu.VMEM(narrow, F32), pltpu.VMEM(narrow, F32),
            pltpu.VMEM(narrow, BF16), pltpu.VMEM(narrow, BF16),
            pltpu.VMEM(narrow, BF16), pltpu.VMEM(narrow, BF16),
            pltpu.VMEM(wide, BF16),
            pltpu.VMEM((STAGES, 2, T), F32), pltpu.VMEM((STAGES, SIDE, 2, T), F32),
            dma((14,)), dma((9,)), dma((9,)), dma((8,)), dma((8,)),
            dma((STAGES, SIDE - 1)), dma((STAGES, SIDE)), dma((KV,)),
        ],
        compiler_params=pltpu.CompilerParams(
            collective_id=0, has_side_effects=True, vmem_limit_bytes=60 * 2**20
        ),
    )(
        queries, keys, values, grad_out, gain_q.reshape(1, T), gain_k.reshape(1, T),
        doc_ids.reshape(1, T), bucket_len.reshape(1, 1),
    )
    done = pl.pallas_call(
        hand_over,
        out_shape=(
            jax.ShapeDtypeStruct(wide, BF16),
            jax.ShapeDtypeStruct(narrow, BF16),
            jax.ShapeDtypeStruct(narrow, BF16),
            jax.ShapeDtypeStruct((1, T), F32),
            jax.ShapeDtypeStruct((1, T), F32),
        ),
        in_specs=[hbm] * 4,
        out_specs=(hbm,) * 5,
        scratch_shapes=[
            pltpu.VMEM(wide, BF16), pltpu.VMEM((2,) + narrow, BF16), pltpu.VMEM((2, T), F32),
            dma((2, PARTS + 4)),
        ],
        compiler_params=pltpu.CompilerParams(vmem_limit_bytes=60 * 2**20),
    )(*outs)
    return done[0], done[1], done[2], done[3].reshape(T), done[4].reshape(T)


def solution(mesh):
    rows = P(("grp", "sp"), None)
    return jax.shard_map(
        body,
        mesh=mesh,
        in_specs=(rows, rows, rows, rows, P(), P(), P(("grp", "sp")), P("grp")),
        out_specs=(rows, rows, rows, P(), P()),
        check_vma=False,
    )
```

```python
import functools
import math

import jax
import jax.numpy as jnp
from jax import lax
from jax.experimental import pallas as pl
from jax.experimental.pallas import tpu as pltpu
from jax.sharding import PartitionSpec as P

MESH = pl.DeviceIdType.MESH
F32 = jnp.float32
BF16 = jnp.bfloat16
eps = 1e-06
masked_score = -1e30
T = 128
HEADS = 32
KV = 4
GROUP = HEADS // KV
SIDES = (8, 8, 8)
PARTS = 4


def ring(value, step, size):
    moved = value + step
    return jnp.where(moved >= size, moved - size, moved)


def places():
    g, s = lax.axis_index("grp"), lax.axis_index("sp")
    x, z_lo, c = g // 8, (g // 2) % 4, g % 2
    y, z_hi = s // 2, s % 2
    plane, column, line = g - 2 * z_lo, s - z_hi, 2 * z_lo

    def along_z(z):
        high = (z >= 4).astype(jnp.int32)
        return (plane + 2 * (z - 4 * high), column + high)

    def along_y(at):
        return (g, at * 2 + z_hi)

    def along_xc(at):
        core = (at >= 4).astype(jnp.int32)
        return ((at - 4 * core) * 8 + line + core, s)

    return ((z_hi * 4 + z_lo, along_z), (y, along_y), (c * 4 + x, along_xc))


def steps(side):
    return sorted(range(1, side), key=lambda step: -min(step, side - step))


def contract(a, b, dims):
    return lax.dot_general(a, b, (dims, ((), ())), preferred_element_type=F32)


def kernel(
    q_hbm, k_hbm, v_hbm, g_hbm, gain_q_hbm, gain_k_hbm, doc_hbm, len_hbm,
    gq_out, gk_out, gv_out, gain_out,
    q_in, g_in, k_in, v_in, gains, doc, length,
    k_halo, v_halo, doc_halo,
    qn, xhat, rfac, kn, kxhat, krfac, bias, live,
    w_own, g_own, own_high, own_sum, own_delta,
    dq, gq_sum, gk_sum, dk_own, dv_own, k_send, v_send, k_back, v_back, gq_stage,
    ar_send, ar_recv,
    in_sem, fwd_send, fwd_recv, ret_send, ret_recv, ars_sem, arr_sem, out_sem,
):
    sp = lax.axis_index("sp")
    grp = lax.axis_index("grp")
    has_prev, has_next = sp > 0, sp < 15
    early = sp % 2 == 0
    nxt, prv = (grp, (sp + 1) % 16), (grp, (sp + 15) % 16)
    scale = 1.0 / math.sqrt(T)

    barrier = pltpu.get_barrier_semaphore()

    def greet(d):
        pl.semaphore_signal(barrier, inc=1, device_id=d, device_id_type=MESH)

    @pl.when(has_next)
    def _():
        greet(nxt)

    @pl.when(has_prev)
    def _():
        greet(prv)

    rows = places()
    peers = [
        {step: device(ring(here, step, side)) for step in steps(side)}
        for (here, device), side in zip(rows, SIDES)
    ]
    for row in peers:
        for d in row.values():
            greet(d)

    loads = [
        (k_hbm, k_in), (v_hbm, v_in), (doc_hbm, doc), (len_hbm, length),
        (gain_q_hbm, gains.at[pl.ds(0, 1)]), (gain_k_hbm, gains.at[pl.ds(1, 1)]),
    ]
    wide = GROUP * T
    for c in range(KV):
        cols = pl.ds(c * wide, wide)
        loads.append((q_hbm.at[:, cols], q_in.at[:, cols]))
        loads.append((g_hbm.at[:, cols], g_in.at[:, cols]))
    loads = [pltpu.make_async_copy(s, d, in_sem.at[i]) for i, (s, d) in enumerate(loads)]

    def head_cols(c):
        return pl.ds(pl.multiple_of(c * T, T), T)

    def start_loads():
        for cp in loads:
            cp.start()

    def forward(c):
        cols = head_cols(c)
        return (
            pltpu.make_async_remote_copy(
                k_hbm.at[:, cols], k_halo.at[:, cols], fwd_send.at[2 * c], fwd_recv.at[2 * c],
                device_id=nxt, device_id_type=MESH,
            ),
            pltpu.make_async_remote_copy(
                v_hbm.at[:, cols], v_halo.at[:, cols], fwd_send.at[2 * c + 1],
                fwd_recv.at[2 * c + 1], device_id=nxt, device_id_type=MESH,
            ),
        )

    def doc_copy():
        return pltpu.make_async_remote_copy(
            doc_hbm, doc_halo, fwd_send.at[2 * KV], fwd_recv.at[2 * KV],
            device_id=nxt, device_id_type=MESH,
        )

    def open_and_send():
        near = has_next.astype(jnp.int32) + has_prev.astype(jnp.int32)
        pl.semaphore_wait(barrier, sum(SIDES) - len(SIDES) + near)

        @pl.when(has_next)
        def _():
            doc_copy().start()
            for c in range(KV):
                for cp in forward(c):
                    cp.start()

    @pl.when(jnp.logical_not(early))
    def _():
        open_and_send()
        start_loads()

    @pl.when(early)
    def _():
        start_loads()

    for cp in loads[:6]:
        cp.wait()
    gain_q, gain_k = gains[0:1, :], gains[1:2, :]

    def factor(x):
        return lax.rsqrt(jnp.mean(x * x, axis=-1, keepdims=True) + eps)

    def norm_keys(raw, c, row):
        x = raw[:, head_cols(c)].astype(F32)
        r = factor(x)
        xr = x * r
        kn[c, row : row + T, :] = (xr * gain_k).astype(BF16)
        kxhat[c, row : row + T, :] = xr
        return r

    for c in range(KV):
        krfac[c] = jnp.broadcast_to(norm_keys(k_in, c, T), (T, T))
    at_t = lax.broadcasted_iota(jnp.int32, (T, T), 1)
    at_s = lax.broadcasted_iota(jnp.int32, (T, T), 0)
    doc_t = jnp.broadcast_to(doc[...].astype(F32), (T, T))
    own = (doc_t == doc_t.T) & (at_s <= at_t)
    bias[T:, :] = jnp.where(own, 0.0, masked_score)
    place = sp * T + lax.broadcasted_iota(jnp.int32, (1, T), 1)
    live[...] = jnp.where(place < length[...], 1.0, 0.0)

    own_bias = jnp.concatenate([bias[T:, :], bias[T:, :]], axis=1)

    def load_grad(h):
        col0 = pl.ds(pl.multiple_of(h * T, T), T)
        col1 = pl.ds(pl.multiple_of(h * T + T, T), T)
        return jnp.concatenate([g_in[:, col0], g_in[:, col1]], axis=0)

    def own_block(c, carry):
        group = pl.ds(pl.multiple_of(c * wide, wide), wide)
        for k, (src, dst) in enumerate(((q_hbm, q_in), (g_hbm, g_in))):
            pltpu.make_async_copy(src.at[:, group], dst.at[:, group], in_sem.at[6 + 2 * c + k]).wait()
        own_key = kn[c, T:, :]
        own_value = v_in[:, head_cols(c)]
        for i in range(GROUP // 2):
            p = c * (GROUP // 2) + i
            for h in (2 * p, 2 * p + 1):
                x = q_in[:, head_cols(h)].astype(F32)
                r = factor(x)
                xr = x * r
                qn[h] = (xr * gain_q).astype(BF16)
                xhat[h] = xr
                rfac[h] = jnp.broadcast_to(r, (T, T))
            query = jnp.concatenate([qn[2 * p], qn[2 * p + 1]], axis=0)
            score = contract(own_key, query, ((1,), (1,))) + own_bias
            high = jnp.max(score, axis=0, keepdims=True)
            weight = jnp.exp((score - high) * scale)
            gatt = contract(own_value, load_grad(2 * p), ((1,), (1,)))
            w_own[p] = weight
            g_own[p] = gatt
            own_high[p] = high
            own_sum[p] = jnp.sum(weight, axis=0, keepdims=True)
            own_delta[p] = jnp.sum(weight * gatt, axis=0, keepdims=True)
        return carry

    lax.fori_loop(0, KV, own_block, 0)

    @pl.when(early)
    def _():
        open_and_send()

    @pl.when(has_prev)
    def _():
        doc_copy().wait_recv()

    @pl.when(jnp.logical_not(has_prev))
    def _():
        doc_halo[...] = jnp.zeros_like(doc_halo)
        k_halo[...] = jnp.zeros_like(k_halo)
        v_halo[...] = jnp.zeros_like(v_halo)

    doc_s = jnp.broadcast_to(doc_halo[...].astype(F32), (T, T)).T
    first = jnp.where(has_prev, 0.0, masked_score)
    bias[:T, :] = jnp.where(doc_s == doc_t, first, masked_score)

    def back(c):
        cols = head_cols(c)
        return (
            pltpu.make_async_remote_copy(
                k_send.at[:, cols], k_back.at[:, cols], ret_send.at[2 * c], ret_recv.at[2 * c],
                device_id=prv, device_id_type=MESH,
            ),
            pltpu.make_async_remote_copy(
                v_send.at[:, cols], v_back.at[:, cols], ret_send.at[2 * c + 1],
                ret_recv.at[2 * c + 1], device_id=prv, device_id_type=MESH,
            ),
        )

    far_bias = jnp.concatenate([bias[:T, :], bias[:T, :]], axis=1)
    alive = jnp.concatenate([live[...], live[...]], axis=1)
    gq_sum[...] = jnp.zeros_like(gq_sum)
    gk_sum[...] = jnp.zeros_like(gk_sum)

    def block(c, carry):
        cols = head_cols(c)

        @pl.when(has_prev)
        def _():
            for cp in forward(c):
                cp.wait_recv()

        norm_keys(k_halo, c, 0)
        key = kn[c]
        value = v_halo[:, cols]
        ds_all, att_all, grads, gains_here = [], [], [], []
        for i in range(GROUP // 2):
            p = c * (GROUP // 2) + i
            h = 2 * p
            query = jnp.concatenate([qn[h], qn[h + 1]], axis=0)
            grad = load_grad(h)
            score = contract(key[:T], query, ((1,), (1,))) + far_bias
            high = jnp.maximum(own_high[p], jnp.max(score, axis=0, keepdims=True))
            weight = jnp.exp((score - high) * scale)
            shrink = jnp.exp((own_high[p] - high) * scale)
            total = shrink * own_sum[p] + jnp.sum(weight, axis=0, keepdims=True)
            inverse = alive / total
            gatt = contract(value, grad, ((1,), (1,)))
            delta = shrink * own_delta[p] + jnp.sum(weight * gatt, axis=0, keepdims=True)
            delta = delta * inverse
            far = weight * inverse
            near = w_own[p] * (shrink * inverse)
            far_ds = (far * (gatt - delta)).astype(BF16)
            near_ds = (near * (g_own[p] - delta)).astype(BF16)
            ds = jnp.concatenate([far_ds, near_ds], axis=0)
            ds_all.append(ds)
            att_all.append(jnp.concatenate([far.astype(BF16), near.astype(BF16)], axis=0))
            grads.append(grad)
            dq2 = contract(ds, key, ((0,), (0,))) * scale
            dq[h] = dq2[:T]
            dq[h + 1] = dq2[T:]
            gains_here.append(dq2[:T] * xhat[h] + dq2[T:] * xhat[h + 1])
        gq_sum[...] += sum(gains_here[1:], gains_here[0])
        queries = qn[pl.ds(c * GROUP, GROUP)].reshape(wide, T)
        dk = contract(jnp.concatenate(ds_all, axis=1), queries, ((1,), (0,))) * scale
        gk_sum[...] += dk * kxhat[c]
        dk_own[:, cols] = dk[T:]
        k_send[:, cols] = dk[:T].astype(BF16)
        dv = contract(jnp.concatenate(att_all, axis=1), jnp.concatenate(grads, axis=0), ((1,), (0,)))
        dv_own[:, cols] = dv[T:]
        v_send[:, cols] = dv[:T].astype(BF16)
        return carry

    lax.fori_loop(0, KV, block, 0)

    sums = jnp.concatenate(
        [
            jnp.sum(gq_sum[...], axis=0, keepdims=True),
            jnp.sum(gk_sum[...], axis=0, keepdims=True),
        ],
        axis=0,
    )

    def exchange(stage):
        (here, _), side = rows[stage], SIDES[stage]
        base = sum(SIDES[:stage])
        return [
            pltpu.make_async_remote_copy(
                ar_send.at[stage], ar_recv.at[base + here], ars_sem.at[base + step],
                arr_sem.at[base + here], device_id=peers[stage][step],
                device_id_type=MESH,
            )
            for step in steps(side)
        ]

    def send_sums(stage, sums):
        ar_send[stage] = sums
        for cp in exchange(stage):
            cp.start()
        ar_recv[sum(SIDES[:stage]) + rows[stage][0]] = sums

    def gather_sums(stage):
        (here, _), side = rows[stage], SIDES[stage]
        base = sum(SIDES[:stage])
        for step in range(1, side):
            at = base + ring(here, step, side)
            pltpu.make_async_copy(ar_recv.at[at], ar_recv.at[at], arr_sem.at[at]).wait()
        total = ar_recv[base]
        for at in range(1, side):
            total = total + ar_recv[base + at]
        return total

    send_sums(0, sums)

    row = rows[0][0]
    last_in = (row == 5) | (row == 6)

    def start_back():
        for c in range(KV):
            for cp in back(c):
                cp.start()

    @pl.when(has_prev & last_in)
    def _():
        start_back()

    def backward(xr, r, gain, up):
        u = gain * up
        return r * (u - xr * jnp.mean(u * xr, axis=-1, keepdims=True))

    def result(c):
        cols = pl.ds(pl.multiple_of(c * wide, wide), wide)
        return pltpu.make_async_copy(gq_stage.at[:, cols], gq_out.at[:, cols], out_sem.at[c])

    def query_grads(c, carry):
        for i in range(GROUP):
            h = c * GROUP + i
            up = backward(xhat[h], rfac[h], gain_q, dq[h])
            gq_stage[:, head_cols(h)] = up.astype(BF16)
        result(c).start()
        return carry

    lax.fori_loop(0, KV, query_grads, 0)

    send_sums(1, gather_sums(0))

    @pl.when(has_prev & jnp.logical_not(last_in))
    def _():
        start_back()

    send_sums(2, gather_sums(1))

    def finish(c, carry):
        cols = head_cols(c)

        @pl.when(has_next)
        def _():
            for cp in back(c):
                cp.wait_recv()
            dk_own[:, cols] = dk_own[:, cols] + k_back[:, cols].astype(F32)
            dv_own[:, cols] = dv_own[:, cols] + v_back[:, cols].astype(F32)

        up = backward(kxhat[c, T:, :], krfac[c], gain_k, dk_own[:, cols])
        gk_out[:, cols] = up.astype(BF16)
        gv_out[:, cols] = dv_own[:, cols].astype(BF16)
        return carry

    lax.fori_loop(0, KV, finish, 0)
    gain_out[...] = gather_sums(2) * (1.0 / math.sqrt(T * 512))

    @pl.when(has_next)
    def _():
        doc_copy().wait_send()
        for c in range(KV):
            for cp in forward(c):
                cp.wait_send()

    @pl.when(has_prev)
    def _():
        for c in range(KV):
            for cp in back(c):
                cp.wait_send()

    for stage in range(len(SIDES)):
        for cp in exchange(stage):
            cp.wait_send()
    for c in range(KV):
        result(c).wait()


def hand_over(gq, gk, gv, gain, gq_out, gk_out, gv_out, gain_q_out, gain_k_out, wide, near, last, sem):
    pairs = [(gk, near.at[0], gk_out), (gv, near.at[1], gv_out)]
    pairs += [
        (gain.at[pl.ds(i, 1)], last.at[pl.ds(i, 1)], out)
        for i, out in enumerate((gain_q_out, gain_k_out))
    ]
    part = T // PARTS
    for i in range(PARTS):
        at = pl.ds(i * part, part)
        pairs.append((gq.at[at], wide.at[at], gq_out.at[at]))
    reads = [pltpu.make_async_copy(a, b, sem.at[0, i]) for i, (a, b, _) in enumerate(pairs)]
    writes = [pltpu.make_async_copy(b, c, sem.at[1, i]) for i, (_, b, c) in enumerate(pairs)]
    for cp in reads:
        cp.start()
    for read, write in zip(reads, writes):
        read.wait()
        write.start()
    for cp in writes:
        cp.wait()


def body(queries, keys, values, grad_out, gain_q, gain_k, doc_ids, bucket_len):
    hbm = pl.BlockSpec(memory_space=pltpu.HBM)
    vmem = pl.BlockSpec(memory_space=pltpu.VMEM)
    wide, narrow = queries.shape, keys.shape
    dma = pltpu.SemaphoreType.DMA
    outs = pl.pallas_call(
        kernel,
        out_shape=(
            jax.ShapeDtypeStruct(wide, BF16),
            jax.ShapeDtypeStruct(narrow, BF16),
            jax.ShapeDtypeStruct(narrow, BF16),
            jax.ShapeDtypeStruct((2, T), F32),
        ),
        in_specs=[hbm] * 8,
        out_specs=(hbm, vmem, vmem, vmem),
        scratch_shapes=[
            pltpu.VMEM(wide, BF16), pltpu.VMEM(wide, BF16),
            pltpu.VMEM(narrow, BF16), pltpu.VMEM(narrow, BF16),
            pltpu.VMEM((2, T), F32), pltpu.VMEM((1, T), jnp.int32), pltpu.VMEM((1, 1), jnp.int32),
            pltpu.VMEM(narrow, BF16), pltpu.VMEM(narrow, BF16), pltpu.VMEM((1, T), jnp.int32),
            pltpu.VMEM((HEADS, T, T), BF16), pltpu.VMEM((HEADS, T, T), F32),
            pltpu.VMEM((HEADS, T, T), F32),
            pltpu.VMEM((KV, 2 * T, T), BF16), pltpu.VMEM((KV, 2 * T, T), F32),
            pltpu.VMEM((KV, T, T), F32),
            pltpu.VMEM((2 * T, T), F32), pltpu.VMEM((1, T), F32),
            pltpu.VMEM((HEADS // 2, T, 2 * T), F32), pltpu.VMEM((HEADS // 2, T, 2 * T), F32),
            pltpu.VMEM((HEADS // 2, 1, 2 * T), F32), pltpu.VMEM((HEADS // 2, 1, 2 * T), F32),
            pltpu.VMEM((HEADS // 2, 1, 2 * T), F32),
            pltpu.VMEM((HEADS, T, T), F32), pltpu.VMEM((T, T), F32), pltpu.VMEM((2 * T, T), F32),
            pltpu.VMEM(narrow, F32), pltpu.VMEM(narrow, F32),
            pltpu.VMEM(narrow, BF16), pltpu.VMEM(narrow, BF16),
            pltpu.VMEM(narrow, BF16), pltpu.VMEM(narrow, BF16),
            pltpu.VMEM(wide, BF16),
            pltpu.VMEM((len(SIDES), 2, T), F32), pltpu.VMEM((sum(SIDES), 2, T), F32),
            dma((14,)), dma((9,)), dma((9,)), dma((8,)), dma((8,)),
            dma((sum(SIDES),)), dma((sum(SIDES),)), dma((KV,)),
        ],
        compiler_params=pltpu.CompilerParams(
            collective_id=0, has_side_effects=True, vmem_limit_bytes=60 * 2**20
        ),
    )(
        queries, keys, values, grad_out, gain_q.reshape(1, T), gain_k.reshape(1, T),
        doc_ids.reshape(1, T), bucket_len.reshape(1, 1),
    )
    done = pl.pallas_call(
        hand_over,
        out_shape=(
            jax.ShapeDtypeStruct(wide, BF16),
            jax.ShapeDtypeStruct(narrow, BF16),
            jax.ShapeDtypeStruct(narrow, BF16),
            jax.ShapeDtypeStruct((1, T), F32),
            jax.ShapeDtypeStruct((1, T), F32),
        ),
        in_specs=[hbm] * 4,
        out_specs=(hbm,) * 5,
        scratch_shapes=[
            pltpu.VMEM(wide, BF16), pltpu.VMEM((2,) + narrow, BF16), pltpu.VMEM((2, T), F32),
            dma((2, PARTS + 4)),
        ],
        compiler_params=pltpu.CompilerParams(vmem_limit_bytes=60 * 2**20),
    )(*outs)
    return done[0], done[1], done[2], done[3].reshape(T), done[4].reshape(T)


def solution(mesh):
    rows = P(("grp", "sp"), None)
    return jax.shard_map(
        body,
        mesh=mesh,
        in_specs=(rows, rows, rows, rows, P(), P(), P(("grp", "sp")), P("grp")),
        out_specs=(rows, rows, rows, P(), P()),
        check_vma=False,
    )
```

```python
import functools
import math

import jax
import jax.numpy as jnp
from jax import lax
from jax.experimental import pallas as pl
from jax.experimental.pallas import tpu as pltpu
from jax.sharding import PartitionSpec as P

MESH = pl.DeviceIdType.MESH
F32 = jnp.float32
BF16 = jnp.bfloat16
eps = 1e-06
masked_score = -1e30
T = 128
HEADS = 32
KV = 4
GROUP = HEADS // KV
SIDES = (8, 8, 8)
PARTS = 4


def ring(value, step, size):
    moved = value + step
    return jnp.where(moved >= size, moved - size, moved)


def places():
    g, s = lax.axis_index("grp"), lax.axis_index("sp")
    x, z_lo, c = g // 8, (g // 2) % 4, g % 2
    y, z_hi = s // 2, s % 2
    plane, column, line = g - 2 * z_lo, s - z_hi, 2 * z_lo

    def along_z(z):
        high = (z >= 4).astype(jnp.int32)
        return (plane + 2 * (z - 4 * high), column + high)

    def along_y(at):
        return (g, at * 2 + z_hi)

    def along_xc(at):
        core = (at >= 4).astype(jnp.int32)
        return ((at - 4 * core) * 8 + line + core, s)

    return ((z_hi * 4 + z_lo, along_z), (y, along_y), (c * 4 + x, along_xc))


def steps(side):
    return sorted(range(1, side), key=lambda step: -min(step, side - step))


def contract(a, b, dims):
    return lax.dot_general(a, b, (dims, ((), ())), preferred_element_type=F32)


def kernel(
    q_hbm, k_hbm, v_hbm, g_hbm, gain_q_hbm, gain_k_hbm, doc_hbm, len_hbm,
    gq_out, gk_out, gv_out, gain_out,
    q_in, g_in, k_in, v_in, gains, doc, length,
    k_halo, v_halo, doc_halo,
    qn, xhat, rfac, kn, kxhat, krfac, bias, live,
    w_own, g_own, own_high, own_sum, own_delta,
    att_low, dq, gq_sum, gk_sum, dk_own, dv_own, k_send, v_send, k_back, v_back, gq_stage,
    ar_send, ar_recv,
    in_sem, fwd_send, fwd_recv, ret_send, ret_recv, ars_sem, arr_sem, out_sem,
):
    sp = lax.axis_index("sp")
    grp = lax.axis_index("grp")
    has_prev, has_next = sp > 0, sp < 15
    early = sp % 2 == 0
    nxt, prv = (grp, (sp + 1) % 16), (grp, (sp + 15) % 16)
    scale = 1.0 / math.sqrt(T)

    barrier = pltpu.get_barrier_semaphore()

    def greet(d):
        pl.semaphore_signal(barrier, inc=1, device_id=d, device_id_type=MESH)

    @pl.when(has_next)
    def _():
        greet(nxt)

    @pl.when(has_prev)
    def _():
        greet(prv)

    rows = places()
    peers = [
        {step: device(ring(here, step, side)) for step in steps(side)}
        for (here, device), side in zip(rows, SIDES)
    ]
    for row in peers:
        for d in row.values():
            greet(d)

    loads = [
        (k_hbm, k_in), (v_hbm, v_in), (doc_hbm, doc), (len_hbm, length),
        (gain_q_hbm, gains.at[pl.ds(0, 1)]), (gain_k_hbm, gains.at[pl.ds(1, 1)]),
    ]
    wide = GROUP * T
    for c in range(KV):
        cols = pl.ds(c * wide, wide)
        loads.append((q_hbm.at[:, cols], q_in.at[:, cols]))
        loads.append((g_hbm.at[:, cols], g_in.at[:, cols]))
    loads = [pltpu.make_async_copy(s, d, in_sem.at[i]) for i, (s, d) in enumerate(loads)]

    def head_cols(c):
        return pl.ds(pl.multiple_of(c * T, T), T)

    def start_loads():
        for cp in loads:
            cp.start()

    def forward(c):
        cols = head_cols(c)
        return (
            pltpu.make_async_remote_copy(
                k_hbm.at[:, cols], k_halo.at[:, cols], fwd_send.at[2 * c], fwd_recv.at[2 * c],
                device_id=nxt, device_id_type=MESH,
            ),
            pltpu.make_async_remote_copy(
                v_hbm.at[:, cols], v_halo.at[:, cols], fwd_send.at[2 * c + 1],
                fwd_recv.at[2 * c + 1], device_id=nxt, device_id_type=MESH,
            ),
        )

    def doc_copy():
        return pltpu.make_async_remote_copy(
            doc_hbm, doc_halo, fwd_send.at[2 * KV], fwd_recv.at[2 * KV],
            device_id=nxt, device_id_type=MESH,
        )

    def open_and_send():
        near = has_next.astype(jnp.int32) + has_prev.astype(jnp.int32)
        pl.semaphore_wait(barrier, sum(SIDES) - len(SIDES) + near)

        @pl.when(has_next)
        def _():
            doc_copy().start()
            for c in range(KV):
                for cp in forward(c):
                    cp.start()

    @pl.when(jnp.logical_not(early))
    def _():
        open_and_send()
        start_loads()

    @pl.when(early)
    def _():
        start_loads()

    for cp in loads[:6]:
        cp.wait()
    gain_q, gain_k = gains[0:1, :], gains[1:2, :]

    def factor(x):
        return lax.rsqrt(jnp.mean(x * x, axis=-1, keepdims=True) + eps)

    def norm_keys(raw, c, row):
        x = raw[:, head_cols(c)].astype(F32)
        r = factor(x)
        xr = x * r
        kn[c, row : row + T, :] = (xr * gain_k).astype(BF16)
        kxhat[c, row : row + T, :] = xr
        return r

    for c in range(KV):
        krfac[c] = jnp.broadcast_to(norm_keys(k_in, c, T), (T, T))
    at_t = lax.broadcasted_iota(jnp.int32, (T, T), 1)
    at_s = lax.broadcasted_iota(jnp.int32, (T, T), 0)
    doc_t = jnp.broadcast_to(doc[...].astype(F32), (T, T))
    own = (doc_t == doc_t.T) & (at_s <= at_t)
    bias[T:, :] = jnp.where(own, 0.0, masked_score)
    place = sp * T + lax.broadcasted_iota(jnp.int32, (1, T), 1)
    live[...] = jnp.where(place < length[...], 1.0, 0.0)

    own_bias = jnp.concatenate([bias[T:, :], bias[T:, :]], axis=1)

    def load_grad(h):
        col0 = pl.ds(pl.multiple_of(h * T, T), T)
        col1 = pl.ds(pl.multiple_of(h * T + T, T), T)
        return jnp.concatenate([g_in[:, col0], g_in[:, col1]], axis=0)

    def own_block(c, carry):
        group = pl.ds(pl.multiple_of(c * wide, wide), wide)
        for k, (src, dst) in enumerate(((q_hbm, q_in), (g_hbm, g_in))):
            pltpu.make_async_copy(src.at[:, group], dst.at[:, group], in_sem.at[6 + 2 * c + k]).wait()
        own_key = kn[c, T:, :]
        own_value = v_in[:, head_cols(c)]
        for i in range(GROUP // 2):
            p = c * (GROUP // 2) + i
            for h in (2 * p, 2 * p + 1):
                x = q_in[:, head_cols(h)].astype(F32)
                r = factor(x)
                xr = x * r
                qn[h] = (xr * gain_q).astype(BF16)
                xhat[h] = xr
                rfac[h] = jnp.broadcast_to(r, (T, T))
            query = jnp.concatenate([qn[2 * p], qn[2 * p + 1]], axis=0)
            score = contract(own_key, query, ((1,), (1,))) + own_bias
            high = jnp.max(score, axis=0, keepdims=True)
            weight = jnp.exp((score - high) * scale)
            gatt = contract(own_value, load_grad(2 * p), ((1,), (1,)))
            w_own[p] = weight
            g_own[p] = gatt
            own_high[p] = high
            own_sum[p] = jnp.sum(weight, axis=0, keepdims=True)
            own_delta[p] = jnp.sum(weight * gatt, axis=0, keepdims=True)
        return carry

    lax.fori_loop(0, KV, own_block, 0)

    @pl.when(early)
    def _():
        open_and_send()

    @pl.when(has_prev)
    def _():
        doc_copy().wait_recv()

    @pl.when(jnp.logical_not(has_prev))
    def _():
        doc_halo[...] = jnp.zeros_like(doc_halo)
        k_halo[...] = jnp.zeros_like(k_halo)
        v_halo[...] = jnp.zeros_like(v_halo)

    doc_s = jnp.broadcast_to(doc_halo[...].astype(F32), (T, T)).T
    first = jnp.where(has_prev, 0.0, masked_score)
    bias[:T, :] = jnp.where(doc_s == doc_t, first, masked_score)

    def back(c):
        cols = head_cols(c)
        return (
            pltpu.make_async_remote_copy(
                k_send.at[:, cols], k_back.at[:, cols], ret_send.at[2 * c], ret_recv.at[2 * c],
                device_id=prv, device_id_type=MESH,
            ),
            pltpu.make_async_remote_copy(
                v_send.at[:, cols], v_back.at[:, cols], ret_send.at[2 * c + 1],
                ret_recv.at[2 * c + 1], device_id=prv, device_id_type=MESH,
            ),
        )

    far_bias = jnp.concatenate([bias[:T, :], bias[:T, :]], axis=1)
    alive = jnp.concatenate([live[...], live[...]], axis=1)
    gq_sum[...] = jnp.zeros_like(gq_sum)
    gk_sum[...] = jnp.zeros_like(gk_sum)

    def block(c, carry):
        cols = head_cols(c)

        @pl.when(has_prev)
        def _():
            for cp in forward(c):
                cp.wait_recv()

        norm_keys(k_halo, c, 0)
        key = kn[c]
        value = v_halo[:, cols]
        ds_all, att_all, gains_here = [], [], []
        for i in range(GROUP // 2):
            p = c * (GROUP // 2) + i
            h = 2 * p
            query = jnp.concatenate([qn[h], qn[h + 1]], axis=0)
            grad = load_grad(h)
            score = contract(key[:T], query, ((1,), (1,))) + far_bias
            high = jnp.maximum(own_high[p], jnp.max(score, axis=0, keepdims=True))
            weight = jnp.exp((score - high) * scale)
            shrink = jnp.exp((own_high[p] - high) * scale)
            total = shrink * own_sum[p] + jnp.sum(weight, axis=0, keepdims=True)
            inverse = alive / total
            gatt = contract(value, grad, ((1,), (1,)))
            delta = shrink * own_delta[p] + jnp.sum(weight * gatt, axis=0, keepdims=True)
            delta = delta * inverse
            far = weight * inverse
            near = w_own[p] * (shrink * inverse)
            far_ds = (far * (gatt - delta)).astype(BF16)
            near_ds = (near * (g_own[p] - delta)).astype(BF16)
            ds = jnp.concatenate([far_ds, near_ds], axis=0)
            ds_all.append(ds)
            att_all.append(jnp.concatenate([far.astype(BF16), near.astype(BF16)], axis=0))
            dq2 = contract(ds, key, ((0,), (0,))) * scale
            dq[h] = dq2[:T]
            dq[h + 1] = dq2[T:]
            gains_here.append(dq2[:T] * xhat[h] + dq2[T:] * xhat[h + 1])
        gq_sum[...] += sum(gains_here[1:], gains_here[0])
        queries = qn[pl.ds(c * GROUP, GROUP)].reshape(wide, T)
        dk = contract(jnp.concatenate(ds_all, axis=1), queries, ((1,), (0,))) * scale
        gk_sum[...] += dk * kxhat[c]
        dk_own[:, cols] = dk[T:]
        k_send[:, cols] = dk[:T].astype(BF16)
        att_low[c] = jnp.concatenate(att_all, axis=1)
        return carry

    lax.fori_loop(0, KV, block, 0)

    def value_sums(c, carry):
        cols = head_cols(c)
        grads = jnp.concatenate([g_in[:, head_cols(c * GROUP + i)] for i in range(GROUP)], axis=0)
        dv = contract(att_low[c], grads, ((1,), (0,)))
        dv_own[:, cols] = dv[T:]
        v_send[:, cols] = dv[:T].astype(BF16)
        return carry

    sums = jnp.concatenate(
        [
            jnp.sum(gq_sum[...], axis=0, keepdims=True),
            jnp.sum(gk_sum[...], axis=0, keepdims=True),
        ],
        axis=0,
    )

    def exchange(stage):
        (here, _), side = rows[stage], SIDES[stage]
        base = sum(SIDES[:stage])
        return [
            pltpu.make_async_remote_copy(
                ar_send.at[stage], ar_recv.at[base + here], ars_sem.at[base + step],
                arr_sem.at[base + here], device_id=peers[stage][step],
                device_id_type=MESH,
            )
            for step in steps(side)
        ]

    def send_sums(stage, sums):
        ar_send[stage] = sums
        for cp in exchange(stage):
            cp.start()
        ar_recv[sum(SIDES[:stage]) + rows[stage][0]] = sums

    def gather_sums(stage):
        (here, _), side = rows[stage], SIDES[stage]
        base = sum(SIDES[:stage])
        for step in range(1, side):
            at = base + ring(here, step, side)
            pltpu.make_async_copy(ar_recv.at[at], ar_recv.at[at], arr_sem.at[at]).wait()
        total = ar_recv[base]
        for at in range(1, side):
            total = total + ar_recv[base + at]
        return total

    send_sums(0, sums)
    lax.fori_loop(0, KV, value_sums, 0)

    row = rows[0][0]
    last_in = (row == 5) | (row == 6)

    def start_back():
        for c in range(KV):
            for cp in back(c):
                cp.start()

    @pl.when(has_prev & last_in)
    def _():
        start_back()

    def backward(xr, r, gain, up):
        u = gain * up
        return r * (u - xr * jnp.mean(u * xr, axis=-1, keepdims=True))

    def result(c):
        cols = pl.ds(pl.multiple_of(c * wide, wide), wide)
        return pltpu.make_async_copy(gq_stage.at[:, cols], gq_out.at[:, cols], out_sem.at[c])

    def query_grads(c, carry):
        for i in range(GROUP):
            h = c * GROUP + i
            up = backward(xhat[h], rfac[h], gain_q, dq[h])
            gq_stage[:, head_cols(h)] = up.astype(BF16)
        result(c).start()
        return carry

    lax.fori_loop(0, KV, query_grads, 0)

    send_sums(1, gather_sums(0))

    @pl.when(has_prev & jnp.logical_not(last_in))
    def _():
        start_back()

    send_sums(2, gather_sums(1))

    def finish(c, carry):
        cols = head_cols(c)

        @pl.when(has_next)
        def _():
            for cp in back(c):
                cp.wait_recv()
            dk_own[:, cols] = dk_own[:, cols] + k_back[:, cols].astype(F32)
            dv_own[:, cols] = dv_own[:, cols] + v_back[:, cols].astype(F32)

        up = backward(kxhat[c, T:, :], krfac[c], gain_k, dk_own[:, cols])
        gk_out[:, cols] = up.astype(BF16)
        gv_out[:, cols] = dv_own[:, cols].astype(BF16)
        return carry

    lax.fori_loop(0, KV, finish, 0)
    gain_out[...] = gather_sums(2) * (1.0 / math.sqrt(T * 512))

    @pl.when(has_next)
    def _():
        doc_copy().wait_send()
        for c in range(KV):
            for cp in forward(c):
                cp.wait_send()

    @pl.when(has_prev)
    def _():
        for c in range(KV):
            for cp in back(c):
                cp.wait_send()

    for stage in range(len(SIDES)):
        for cp in exchange(stage):
            cp.wait_send()
    for c in range(KV):
        result(c).wait()


def hand_over(gq, gk, gv, gain, gq_out, gk_out, gv_out, gain_q_out, gain_k_out, wide, near, last, sem):
    pairs = [(gk, near.at[0], gk_out), (gv, near.at[1], gv_out)]
    pairs += [
        (gain.at[pl.ds(i, 1)], last.at[pl.ds(i, 1)], out)
        for i, out in enumerate((gain_q_out, gain_k_out))
    ]
    part = T // PARTS
    for i in range(PARTS):
        at = pl.ds(i * part, part)
        pairs.append((gq.at[at], wide.at[at], gq_out.at[at]))
    reads = [pltpu.make_async_copy(a, b, sem.at[0, i]) for i, (a, b, _) in enumerate(pairs)]
    writes = [pltpu.make_async_copy(b, c, sem.at[1, i]) for i, (_, b, c) in enumerate(pairs)]
    for cp in reads:
        cp.start()
    for read, write in zip(reads, writes):
        read.wait()
        write.start()
    for cp in writes:
        cp.wait()


def body(queries, keys, values, grad_out, gain_q, gain_k, doc_ids, bucket_len):
    hbm = pl.BlockSpec(memory_space=pltpu.HBM)
    vmem = pl.BlockSpec(memory_space=pltpu.VMEM)
    wide, narrow = queries.shape, keys.shape
    dma = pltpu.SemaphoreType.DMA
    outs = pl.pallas_call(
        kernel,
        out_shape=(
            jax.ShapeDtypeStruct(wide, BF16),
            jax.ShapeDtypeStruct(narrow, BF16),
            jax.ShapeDtypeStruct(narrow, BF16),
            jax.ShapeDtypeStruct((2, T), F32),
        ),
        in_specs=[hbm] * 8,
        out_specs=(hbm, vmem, vmem, vmem),
        scratch_shapes=[
            pltpu.VMEM(wide, BF16), pltpu.VMEM(wide, BF16),
            pltpu.VMEM(narrow, BF16), pltpu.VMEM(narrow, BF16),
            pltpu.VMEM((2, T), F32), pltpu.VMEM((1, T), jnp.int32), pltpu.VMEM((1, 1), jnp.int32),
            pltpu.VMEM(narrow, BF16), pltpu.VMEM(narrow, BF16), pltpu.VMEM((1, T), jnp.int32),
            pltpu.VMEM((HEADS, T, T), BF16), pltpu.VMEM((HEADS, T, T), F32),
            pltpu.VMEM((HEADS, T, T), F32),
            pltpu.VMEM((KV, 2 * T, T), BF16), pltpu.VMEM((KV, 2 * T, T), F32),
            pltpu.VMEM((KV, T, T), F32),
            pltpu.VMEM((2 * T, T), F32), pltpu.VMEM((1, T), F32),
            pltpu.VMEM((HEADS // 2, T, 2 * T), F32), pltpu.VMEM((HEADS // 2, T, 2 * T), F32),
            pltpu.VMEM((HEADS // 2, 1, 2 * T), F32), pltpu.VMEM((HEADS // 2, 1, 2 * T), F32),
            pltpu.VMEM((HEADS // 2, 1, 2 * T), F32),
            pltpu.VMEM((KV, 2 * T, GROUP * T), BF16),
            pltpu.VMEM((HEADS, T, T), F32), pltpu.VMEM((T, T), F32), pltpu.VMEM((2 * T, T), F32),
            pltpu.VMEM(narrow, F32), pltpu.VMEM(narrow, F32),
            pltpu.VMEM(narrow, BF16), pltpu.VMEM(narrow, BF16),
            pltpu.VMEM(narrow, BF16), pltpu.VMEM(narrow, BF16),
            pltpu.VMEM(wide, BF16),
            pltpu.VMEM((len(SIDES), 2, T), F32), pltpu.VMEM((sum(SIDES), 2, T), F32),
            dma((14,)), dma((9,)), dma((9,)), dma((8,)), dma((8,)),
            dma((sum(SIDES),)), dma((sum(SIDES),)), dma((KV,)),
        ],
        compiler_params=pltpu.CompilerParams(
            collective_id=0, has_side_effects=True, vmem_limit_bytes=60 * 2**20
        ),
    )(
        queries, keys, values, grad_out, gain_q.reshape(1, T), gain_k.reshape(1, T),
        doc_ids.reshape(1, T), bucket_len.reshape(1, 1),
    )
    done = pl.pallas_call(
        hand_over,
        out_shape=(
            jax.ShapeDtypeStruct(wide, BF16),
            jax.ShapeDtypeStruct(narrow, BF16),
            jax.ShapeDtypeStruct(narrow, BF16),
            jax.ShapeDtypeStruct((1, T), F32),
            jax.ShapeDtypeStruct((1, T), F32),
        ),
        in_specs=[hbm] * 4,
        out_specs=(hbm,) * 5,
        scratch_shapes=[
            pltpu.VMEM(wide, BF16), pltpu.VMEM((2,) + narrow, BF16), pltpu.VMEM((2, T), F32),
            dma((2, PARTS + 4)),
        ],
        compiler_params=pltpu.CompilerParams(vmem_limit_bytes=60 * 2**20),
    )(*outs)
    return done[0], done[1], done[2], done[3].reshape(T), done[4].reshape(T)


def solution(mesh):
    rows = P(("grp", "sp"), None)
    return jax.shard_map(
        body,
        mesh=mesh,
        in_specs=(rows, rows, rows, rows, P(), P(), P(("grp", "sp")), P("grp")),
        out_specs=(rows, rows, rows, P(), P()),
        check_vma=False,
    )
```

```python
import functools
import math

import jax
import jax.numpy as jnp
from jax import lax
from jax.experimental import pallas as pl
from jax.experimental.pallas import tpu as pltpu
from jax.sharding import PartitionSpec as P

MESH = pl.DeviceIdType.MESH
F32 = jnp.float32
BF16 = jnp.bfloat16
eps = 1e-06
masked_score = -1e30
T = 128
HEADS = 32
KV = 4
GROUP = HEADS // KV
SIDES = (8, 8, 8)
PARTS = 4


def ring(value, step, size):
    moved = value + step
    return jnp.where(moved >= size, moved - size, moved)


def places():
    g, s = lax.axis_index("grp"), lax.axis_index("sp")
    x, z_lo, c = g // 8, (g // 2) % 4, g % 2
    y, z_hi = s // 2, s % 2
    plane, column, line = g - 2 * z_lo, s - z_hi, 2 * z_lo

    def along_z(z):
        high = (z >= 4).astype(jnp.int32)
        return (plane + 2 * (z - 4 * high), column + high)

    def along_y(at):
        return (g, at * 2 + z_hi)

    def along_xc(at):
        core = (at >= 4).astype(jnp.int32)
        return ((at - 4 * core) * 8 + line + core, s)

    return ((z_hi * 4 + z_lo, along_z), (y, along_y), (c * 4 + x, along_xc))


def steps(side):
    return sorted(range(1, side), key=lambda step: -min(step, side - step))


def contract(a, b, dims):
    return lax.dot_general(a, b, (dims, ((), ())), preferred_element_type=F32)


def kernel(
    q_hbm, k_hbm, v_hbm, g_hbm, gain_q_hbm, gain_k_hbm, doc_hbm, len_hbm,
    gq_out, gk_out, gv_out, gain_out,
    q_in, g_in, k_in, v_in, gains, doc, length,
    k_halo, v_halo, doc_halo,
    qn, xhat, rfac, kn, kxhat, krfac, bias, live,
    w_own, g_own, own_high, own_sum, own_delta,
    att_low, dq, gq_sum, gk_sum, dk_own, dv_own, k_send, v_send, k_back, v_back, gq_stage,
    ar_send, ar_recv,
    in_sem, fwd_send, fwd_recv, ret_send, ret_recv, ars_sem, arr_sem, out_sem,
):
    sp = lax.axis_index("sp")
    grp = lax.axis_index("grp")
    has_prev, has_next = sp > 0, sp < 15
    early = sp % 2 == 0
    nxt, prv = (grp, (sp + 1) % 16), (grp, (sp + 15) % 16)
    scale = 1.0 / math.sqrt(T)

    barrier = pltpu.get_barrier_semaphore()

    def greet(d):
        pl.semaphore_signal(barrier, inc=1, device_id=d, device_id_type=MESH)

    @pl.when(has_next)
    def _():
        greet(nxt)

    @pl.when(has_prev)
    def _():
        greet(prv)

    rows = places()
    peers = [
        {step: device(ring(here, step, side)) for step in steps(side)}
        for (here, device), side in zip(rows, SIDES)
    ]
    for row in peers:
        for d in row.values():
            greet(d)

    loads = [
        (k_hbm, k_in), (v_hbm, v_in), (doc_hbm, doc), (len_hbm, length),
        (gain_q_hbm, gains.at[pl.ds(0, 1)]), (gain_k_hbm, gains.at[pl.ds(1, 1)]),
    ]
    wide = GROUP * T
    for c in range(KV):
        cols = pl.ds(c * wide, wide)
        loads.append((q_hbm.at[:, cols], q_in.at[:, cols]))
        loads.append((g_hbm.at[:, cols], g_in.at[:, cols]))
    loads = [pltpu.make_async_copy(s, d, in_sem.at[i]) for i, (s, d) in enumerate(loads)]

    def head_cols(c):
        return pl.ds(pl.multiple_of(c * T, T), T)

    def start_loads():
        for cp in loads:
            cp.start()

    def forward(c):
        cols = head_cols(c)
        return (
            pltpu.make_async_remote_copy(
                k_hbm.at[:, cols], k_halo.at[:, cols], fwd_send.at[2 * c], fwd_recv.at[2 * c],
                device_id=nxt, device_id_type=MESH,
            ),
            pltpu.make_async_remote_copy(
                v_hbm.at[:, cols], v_halo.at[:, cols], fwd_send.at[2 * c + 1],
                fwd_recv.at[2 * c + 1], device_id=nxt, device_id_type=MESH,
            ),
        )

    def doc_copy():
        return pltpu.make_async_remote_copy(
            doc_hbm, doc_halo, fwd_send.at[2 * KV], fwd_recv.at[2 * KV],
            device_id=nxt, device_id_type=MESH,
        )

    def open_and_send():
        near = has_next.astype(jnp.int32) + has_prev.astype(jnp.int32)
        pl.semaphore_wait(barrier, sum(SIDES) - len(SIDES) + near)

        @pl.when(has_next)
        def _():
            doc_copy().start()
            for c in range(KV):
                for cp in forward(c):
                    cp.start()

    @pl.when(jnp.logical_not(early))
    def _():
        open_and_send()
        start_loads()

    @pl.when(early)
    def _():
        start_loads()

    for cp in loads[:6]:
        cp.wait()
    gain_q, gain_k = gains[0:1, :], gains[1:2, :]

    def factor(x):
        return lax.rsqrt(jnp.mean(x * x, axis=-1, keepdims=True) + eps)

    def norm_keys(raw, c, row):
        x = raw[:, head_cols(c)].astype(F32)
        r = factor(x)
        xr = x * r
        kn[c, row : row + T, :] = (xr * gain_k).astype(BF16)
        kxhat[c, row : row + T, :] = xr
        return r

    for c in range(KV):
        krfac[c] = jnp.broadcast_to(norm_keys(k_in, c, T), (T, T))
    at_t = lax.broadcasted_iota(jnp.int32, (T, T), 1)
    at_s = lax.broadcasted_iota(jnp.int32, (T, T), 0)
    doc_t = jnp.broadcast_to(doc[...].astype(F32), (T, T))
    own = (doc_t == doc_t.T) & (at_s <= at_t)
    bias[T:, :] = jnp.where(own, 0.0, masked_score)
    place = sp * T + lax.broadcasted_iota(jnp.int32, (1, T), 1)
    live[...] = jnp.where(place < length[...], 1.0, 0.0)

    own_bias = jnp.concatenate([bias[T:, :], bias[T:, :]], axis=1)

    def load_grad(h):
        col0 = pl.ds(pl.multiple_of(h * T, T), T)
        col1 = pl.ds(pl.multiple_of(h * T + T, T), T)
        return jnp.concatenate([g_in[:, col0], g_in[:, col1]], axis=0)

    def own_block(c, carry):
        group = pl.ds(pl.multiple_of(c * wide, wide), wide)
        for k, (src, dst) in enumerate(((q_hbm, q_in), (g_hbm, g_in))):
            pltpu.make_async_copy(src.at[:, group], dst.at[:, group], in_sem.at[6 + 2 * c + k]).wait()
        own_key = kn[c, T:, :]
        own_value = v_in[:, head_cols(c)]
        for i in range(GROUP // 2):
            p = c * (GROUP // 2) + i
            for h in (2 * p, 2 * p + 1):
                x = q_in[:, head_cols(h)].astype(F32)
                r = factor(x)
                xr = x * r
                qn[h] = (xr * gain_q).astype(BF16)
                xhat[h] = xr
                rfac[h] = jnp.broadcast_to(r, (T, T))
            query = jnp.concatenate([qn[2 * p], qn[2 * p + 1]], axis=0)
            score = contract(own_key, query, ((1,), (1,))) + own_bias
            high = jnp.max(score, axis=0, keepdims=True)
            weight = jnp.exp((score - high) * scale)
            gatt = contract(own_value, load_grad(2 * p), ((1,), (1,)))
            w_own[p] = weight
            g_own[p] = gatt
            own_high[p] = high
            own_sum[p] = jnp.sum(weight, axis=0, keepdims=True)
            own_delta[p] = jnp.sum(weight * gatt, axis=0, keepdims=True)
        return carry

    lax.fori_loop(0, KV, own_block, 0)

    @pl.when(early)
    def _():
        open_and_send()

    @pl.when(has_prev)
    def _():
        doc_copy().wait_recv()

    @pl.when(jnp.logical_not(has_prev))
    def _():
        doc_halo[...] = jnp.zeros_like(doc_halo)
        k_halo[...] = jnp.zeros_like(k_halo)
        v_halo[...] = jnp.zeros_like(v_halo)

    doc_s = jnp.broadcast_to(doc_halo[...].astype(F32), (T, T)).T
    first = jnp.where(has_prev, 0.0, masked_score)
    bias[:T, :] = jnp.where(doc_s == doc_t, first, masked_score)

    def back(c):
        cols = head_cols(c)
        return (
            pltpu.make_async_remote_copy(
                k_send.at[:, cols], k_back.at[:, cols], ret_send.at[2 * c], ret_recv.at[2 * c],
                device_id=prv, device_id_type=MESH,
            ),
            pltpu.make_async_remote_copy(
                v_send.at[:, cols], v_back.at[:, cols], ret_send.at[2 * c + 1],
                ret_recv.at[2 * c + 1], device_id=prv, device_id_type=MESH,
            ),
        )

    far_bias = jnp.concatenate([bias[:T, :], bias[:T, :]], axis=1)
    alive = jnp.concatenate([live[...], live[...]], axis=1)
    gq_sum[...] = jnp.zeros_like(gq_sum)
    gk_sum[...] = jnp.zeros_like(gk_sum)

    def block(c, carry):
        cols = head_cols(c)

        @pl.when(has_prev)
        def _():
            for cp in forward(c):
                cp.wait_recv()

        norm_keys(k_halo, c, 0)
        key = kn[c]
        value = v_halo[:, cols]
        ds_all, att_all, gains_here = [], [], []
        for i in range(GROUP // 2):
            p = c * (GROUP // 2) + i
            h = 2 * p
            query = jnp.concatenate([qn[h], qn[h + 1]], axis=0)
            grad = load_grad(h)
            score = contract(key[:T], query, ((1,), (1,))) + far_bias
            high = jnp.maximum(own_high[p], jnp.max(score, axis=0, keepdims=True))
            weight = jnp.exp((score - high) * scale)
            shrink = jnp.exp((own_high[p] - high) * scale)
            total = shrink * own_sum[p] + jnp.sum(weight, axis=0, keepdims=True)
            inverse = alive / total
            gatt = contract(value, grad, ((1,), (1,)))
            delta = shrink * own_delta[p] + jnp.sum(weight * gatt, axis=0, keepdims=True)
            delta = delta * inverse
            far = weight * inverse
            near = w_own[p] * (shrink * inverse)
            far_ds = (far * (gatt - delta)).astype(BF16)
            near_ds = (near * (g_own[p] - delta)).astype(BF16)
            ds = jnp.concatenate([far_ds, near_ds], axis=0)
            ds_all.append(ds)
            att_all.append(jnp.concatenate([far.astype(BF16), near.astype(BF16)], axis=0))
            dq2 = contract(ds, key, ((0,), (0,))) * scale
            dq[h] = dq2[:T]
            dq[h + 1] = dq2[T:]
            gains_here.append(dq2[:T] * xhat[h] + dq2[T:] * xhat[h + 1])
        gq_sum[...] += sum(gains_here[1:], gains_here[0])
        queries = qn[pl.ds(c * GROUP, GROUP)].reshape(wide, T)
        dk = contract(jnp.concatenate(ds_all, axis=1), queries, ((1,), (0,))) * scale
        gk_sum[...] += dk * kxhat[c]
        dk_own[:, cols] = dk[T:]
        k_send[:, cols] = dk[:T].astype(BF16)
        att_low[c] = jnp.concatenate(att_all, axis=1)
        return carry

    lax.fori_loop(0, KV, block, 0)

    def value_sums(c, carry):
        cols = head_cols(c)
        grads = jnp.concatenate([g_in[:, head_cols(c * GROUP + i)] for i in range(GROUP)], axis=0)
        dv = contract(att_low[c], grads, ((1,), (0,)))
        dv_own[:, cols] = dv[T:]
        v_send[:, cols] = dv[:T].astype(BF16)
        return carry

    sums = jnp.concatenate(
        [
            jnp.sum(gq_sum[...], axis=0, keepdims=True),
            jnp.sum(gk_sum[...], axis=0, keepdims=True),
        ],
        axis=0,
    )

    def exchange(stage):
        (here, _), side = rows[stage], SIDES[stage]
        base = sum(SIDES[:stage])
        return [
            pltpu.make_async_remote_copy(
                ar_send.at[stage], ar_recv.at[base + here], ars_sem.at[base + step],
                arr_sem.at[base + here], device_id=peers[stage][step],
                device_id_type=MESH,
            )
            for step in steps(side)
        ]

    def send_sums(stage, sums):
        ar_send[stage] = sums
        for cp in exchange(stage):
            cp.start()
        ar_recv[sum(SIDES[:stage]) + rows[stage][0]] = sums

    def gather_sums(stage):
        (here, _), side = rows[stage], SIDES[stage]
        base = sum(SIDES[:stage])
        for step in range(1, side):
            at = base + ring(here, step, side)
            pltpu.make_async_copy(ar_recv.at[at], ar_recv.at[at], arr_sem.at[at]).wait()
        total = ar_recv[base]
        for at in range(1, side):
            total = total + ar_recv[base + at]
        return total

    send_sums(0, sums)

    row = rows[0][0]
    last_in = (row == 5) | (row == 6)

    def start_back():
        for c in range(KV):
            for cp in back(c):
                cp.start()

    def start_part(part):
        for c in range(KV):
            back(c)[part].start()

    @pl.when(has_prev & last_in)
    def _():
        start_part(0)

    lax.fori_loop(0, KV, value_sums, 0)

    @pl.when(has_prev & last_in)
    def _():
        start_part(1)

    def backward(xr, r, gain, up):
        u = gain * up
        return r * (u - xr * jnp.mean(u * xr, axis=-1, keepdims=True))

    def result(c):
        cols = pl.ds(pl.multiple_of(c * wide, wide), wide)
        return pltpu.make_async_copy(gq_stage.at[:, cols], gq_out.at[:, cols], out_sem.at[c])

    def query_grads(c, carry):
        for i in range(GROUP):
            h = c * GROUP + i
            up = backward(xhat[h], rfac[h], gain_q, dq[h])
            gq_stage[:, head_cols(h)] = up.astype(BF16)
        result(c).start()
        return carry

    lax.fori_loop(0, KV, query_grads, 0)

    send_sums(1, gather_sums(0))

    @pl.when(has_prev & jnp.logical_not(last_in))
    def _():
        start_back()

    send_sums(2, gather_sums(1))

    def finish(c, carry):
        cols = head_cols(c)

        @pl.when(has_next)
        def _():
            for cp in back(c):
                cp.wait_recv()
            dk_own[:, cols] = dk_own[:, cols] + k_back[:, cols].astype(F32)
            dv_own[:, cols] = dv_own[:, cols] + v_back[:, cols].astype(F32)

        up = backward(kxhat[c, T:, :], krfac[c], gain_k, dk_own[:, cols])
        gk_out[:, cols] = up.astype(BF16)
        gv_out[:, cols] = dv_own[:, cols].astype(BF16)
        return carry

    lax.fori_loop(0, KV, finish, 0)
    gain_out[...] = gather_sums(2) * (1.0 / math.sqrt(T * 512))

    @pl.when(has_next)
    def _():
        doc_copy().wait_send()
        for c in range(KV):
            for cp in forward(c):
                cp.wait_send()

    @pl.when(has_prev)
    def _():
        for c in range(KV):
            for cp in back(c):
                cp.wait_send()

    for stage in range(len(SIDES)):
        for cp in exchange(stage):
            cp.wait_send()
    for c in range(KV):
        result(c).wait()


def hand_over(gq, gk, gv, gain, gq_out, gk_out, gv_out, gain_q_out, gain_k_out, wide, near, last, sem):
    pairs = [(gk, near.at[0], gk_out), (gv, near.at[1], gv_out)]
    pairs += [
        (gain.at[pl.ds(i, 1)], last.at[pl.ds(i, 1)], out)
        for i, out in enumerate((gain_q_out, gain_k_out))
    ]
    part = T // PARTS
    for i in range(PARTS):
        at = pl.ds(i * part, part)
        pairs.append((gq.at[at], wide.at[at], gq_out.at[at]))
    reads = [pltpu.make_async_copy(a, b, sem.at[0, i]) for i, (a, b, _) in enumerate(pairs)]
    writes = [pltpu.make_async_copy(b, c, sem.at[1, i]) for i, (_, b, c) in enumerate(pairs)]
    for cp in reads:
        cp.start()
    for read, write in zip(reads, writes):
        read.wait()
        write.start()
    for cp in writes:
        cp.wait()


def body(queries, keys, values, grad_out, gain_q, gain_k, doc_ids, bucket_len):
    hbm = pl.BlockSpec(memory_space=pltpu.HBM)
    vmem = pl.BlockSpec(memory_space=pltpu.VMEM)
    wide, narrow = queries.shape, keys.shape
    dma = pltpu.SemaphoreType.DMA
    outs = pl.pallas_call(
        kernel,
        out_shape=(
            jax.ShapeDtypeStruct(wide, BF16),
            jax.ShapeDtypeStruct(narrow, BF16),
            jax.ShapeDtypeStruct(narrow, BF16),
            jax.ShapeDtypeStruct((2, T), F32),
        ),
        in_specs=[hbm] * 8,
        out_specs=(hbm, vmem, vmem, vmem),
        scratch_shapes=[
            pltpu.VMEM(wide, BF16), pltpu.VMEM(wide, BF16),
            pltpu.VMEM(narrow, BF16), pltpu.VMEM(narrow, BF16),
            pltpu.VMEM((2, T), F32), pltpu.VMEM((1, T), jnp.int32), pltpu.VMEM((1, 1), jnp.int32),
            pltpu.VMEM(narrow, BF16), pltpu.VMEM(narrow, BF16), pltpu.VMEM((1, T), jnp.int32),
            pltpu.VMEM((HEADS, T, T), BF16), pltpu.VMEM((HEADS, T, T), F32),
            pltpu.VMEM((HEADS, T, T), F32),
            pltpu.VMEM((KV, 2 * T, T), BF16), pltpu.VMEM((KV, 2 * T, T), F32),
            pltpu.VMEM((KV, T, T), F32),
            pltpu.VMEM((2 * T, T), F32), pltpu.VMEM((1, T), F32),
            pltpu.VMEM((HEADS // 2, T, 2 * T), F32), pltpu.VMEM((HEADS // 2, T, 2 * T), F32),
            pltpu.VMEM((HEADS // 2, 1, 2 * T), F32), pltpu.VMEM((HEADS // 2, 1, 2 * T), F32),
            pltpu.VMEM((HEADS // 2, 1, 2 * T), F32),
            pltpu.VMEM((KV, 2 * T, GROUP * T), BF16),
            pltpu.VMEM((HEADS, T, T), F32), pltpu.VMEM((T, T), F32), pltpu.VMEM((2 * T, T), F32),
            pltpu.VMEM(narrow, F32), pltpu.VMEM(narrow, F32),
            pltpu.VMEM(narrow, BF16), pltpu.VMEM(narrow, BF16),
            pltpu.VMEM(narrow, BF16), pltpu.VMEM(narrow, BF16),
            pltpu.VMEM(wide, BF16),
            pltpu.VMEM((len(SIDES), 2, T), F32), pltpu.VMEM((sum(SIDES), 2, T), F32),
            dma((14,)), dma((9,)), dma((9,)), dma((8,)), dma((8,)),
            dma((sum(SIDES),)), dma((sum(SIDES),)), dma((KV,)),
        ],
        compiler_params=pltpu.CompilerParams(
            collective_id=0, has_side_effects=True, vmem_limit_bytes=60 * 2**20
        ),
    )(
        queries, keys, values, grad_out, gain_q.reshape(1, T), gain_k.reshape(1, T),
        doc_ids.reshape(1, T), bucket_len.reshape(1, 1),
    )
    done = pl.pallas_call(
        hand_over,
        out_shape=(
            jax.ShapeDtypeStruct(wide, BF16),
            jax.ShapeDtypeStruct(narrow, BF16),
            jax.ShapeDtypeStruct(narrow, BF16),
            jax.ShapeDtypeStruct((1, T), F32),
            jax.ShapeDtypeStruct((1, T), F32),
        ),
        in_specs=[hbm] * 4,
        out_specs=(hbm,) * 5,
        scratch_shapes=[
            pltpu.VMEM(wide, BF16), pltpu.VMEM((2,) + narrow, BF16), pltpu.VMEM((2, T), F32),
            dma((2, PARTS + 4)),
        ],
        compiler_params=pltpu.CompilerParams(vmem_limit_bytes=60 * 2**20),
    )(*outs)
    return done[0], done[1], done[2], done[3].reshape(T), done[4].reshape(T)


def solution(mesh):
    rows = P(("grp", "sp"), None)
    return jax.shard_map(
        body,
        mesh=mesh,
        in_specs=(rows, rows, rows, rows, P(), P(), P(("grp", "sp")), P("grp")),
        out_specs=(rows, rows, rows, P(), P()),
        check_vma=False,
    )
```
